512 devices in a mesh: seq: 128 (over y, z, core), head: 4 (over x).
Axes of the slice: x: 4, y: 8, z: 8, core: 2. Of those that a mesh axis runs over, the one named last changes fastest.
Arguments:
- queries: bfloat16 [65536, 4096], P('seq', 'head'), may hold values from -7 to 7
- keys: bfloat16 [65536, 1024], P('seq', 'head'), may hold values from -5 to 5
- values: bfloat16 [65536, 1024], P('seq', 'head'), may hold values from -6 to 6
- picks: int32 [65536, 2], P('seq'), may hold values from -1 to 126, as said below
- out_weight: bfloat16 [4096, 4096], P('seq', 'head'), may hold values from -0.09375 to 0.09375
Outputs:
- mixed: bfloat16 [65536, 4096], P('seq', 'head')
The draws below stay inside these ranges and needn't reach their ends.
Inputs may be any that keep to these rules, and one draw needn't show every extreme that they name: `picks`: for the tokens of block d, every entry is -1 or a block number below d; a row's two entries differ unless both are -1; a row naming one block has it first, and a row naming two has the lower first; each earlier block is named by exactly 6 of block d's rows.
All inputs are finite; a program needn't handle non-finite values.
Results may differ from the reference program's by a relative error of at most 0.0054.
Values may be sent and summed in bfloat16 or wider, within the bound.
A program may use at most 64 MiB of HBM per device.

```python
import math
import jax
import jax.numpy as jnp
from jax import lax

D = 4096
QUERY_HEADS = 32
KEY_VALUE_HEADS = 8
HEAD_SIZE = 128
BLOCK_TOKENS = 512
CAP = 6
SEQUENCE_TOKENS = 65536


def shared_keys(key):
    return jax.random.normal(key, (SEQUENCE_TOKENS, KEY_VALUE_HEADS * HEAD_SIZE), jnp.float32)


def draw_keys(key, part):
    key_base = shared_keys(key)
    return jnp.clip(key_base, -5.0, 5.0).astype(jnp.bfloat16)


def draw_queries(key, part):
    key = jax.random.fold_in(key, 12)
    random_part = jax.random.normal(key, (SEQUENCE_TOKENS, QUERY_HEADS * HEAD_SIZE), jnp.float32)
    return jnp.clip(random_part, -7.0, 7.0).astype(jnp.bfloat16)


def draw_picks(key, part):
    key = jax.random.fold_in(key, 13)

    def one_block(holding_block):
        shuffle = jax.random.permutation(jax.random.fold_in(key, holding_block), BLOCK_TOKENS)
        position = jnp.argsort(shuffle).astype(jnp.int32)
        item_index = jnp.arange(2, dtype=jnp.int32)[None, :] * BLOCK_TOKENS + position[:, None]
        return jnp.where(item_index < CAP * holding_block, item_index // CAP, -1).astype(jnp.int32)
    return jax.lax.map(one_block, jnp.arange(SEQUENCE_TOKENS // BLOCK_TOKENS, dtype=jnp.int32)).reshape(SEQUENCE_TOKENS, 2)


def steps_of(stream_key, shape, split, smallest, high):
    loudness, own = 1.0, jax.random.fold_in(stream_key, 6)
    for dim, parts in split:
        draws = jnp.exp(jax.random.uniform(jax.random.fold_in(own, dim), (parts,), jnp.float32, smallest / len(split), high / len(split)))
        loudness = loudness * jnp.repeat(draws, shape[dim] // parts).reshape([-1 if axis == dim else 1 for axis in range(len(shape))])
    return loudness


def gaussian(key, extent, deviation, reach, split=(), kind=jnp.bfloat16):
    values = jax.random.normal(key, extent, jnp.float32) * deviation
    if len(split) > 0:
        values = steps_of(key, extent, split, -0.22, 0.18) * values
    return jnp.clip(values, min=-reach, max=reach).astype(kind)


def setup_inputs(seed: int = 0) -> dict:
    seeds = jax.random.split(jax.random.key(seed), 6)
    queries = draw_queries(jax.random.fold_in(seeds[5], 71), 0)
    keys = draw_keys(jax.random.fold_in(seeds[5], 71), 0)
    values = gaussian(seeds[2], (SEQUENCE_TOKENS, KEY_VALUE_HEADS * HEAD_SIZE), 1.0, 6.0, ((0, 128), (1, 4)))
    picks = draw_picks(jax.random.fold_in(seeds[5], 71), 0)
    out_weight = gaussian(seeds[4], (QUERY_HEADS * HEAD_SIZE, D), (QUERY_HEADS * HEAD_SIZE) ** -0.5, 0.09375, ((0, 128), (1, 4)))
    return dict(queries=queries, keys=keys, values=values, picks=picks, out_weight=out_weight)


NEG_FILL = -1e+30

def own_partial(query_matrix, key_matrix, value_matrix, first_row, score_scale):
    row_count = query_matrix.shape[0]
    key_count = key_matrix.shape[0]
    scores = jnp.einsum('qjgd,kjd->jgqk', query_matrix, key_matrix) * score_scale
    visible = jnp.arange(key_count)[None, :] <= (first_row + jnp.arange(row_count))[:, None]
    scores = jnp.where(visible, scores, NEG_FILL)
    peak_score = lax.optimization_barrier(jnp.max(scores, axis=-1))
    weights = jnp.where(visible, jnp.exp(scores - peak_score[..., None]), 0.0)
    totals = lax.optimization_barrier(jnp.sum(weights, axis=-1))
    rounded = lax.optimization_barrier(weights.astype(jnp.bfloat16)).astype(jnp.float32)
    mixed_rows = jnp.einsum('jgqk,kjd->qjgd', rounded, value_matrix)
    mixed_rows = mixed_rows / jnp.transpose(totals, (2, 0, 1))[..., None]
    return (mixed_rows.reshape(row_count, -1, HEAD_SIZE), jnp.transpose(peak_score, (2, 0, 1)).reshape(row_count, -1), jnp.transpose(totals, (2, 0, 1)).reshape(row_count, -1))

def merge_parts(own_out, own_peak, own_total, pick_out, pick_peak, pick_total, live_rows):
    live_mask = live_rows[:, :, None]
    pick_peak = jnp.where(live_mask, pick_peak, own_peak[:, None, :])
    summit = jnp.maximum(own_peak, lax.optimization_barrier(jnp.max(pick_peak, axis=1)))
    own_weight = own_total * jnp.exp(own_peak - summit)
    pick_weight = jnp.where(live_mask, pick_total * jnp.exp(pick_peak - summit[:, None, :]), 0.0)
    weighted_sum = own_weight[..., None] * own_out + lax.optimization_barrier(jnp.sum(pick_weight[..., None] * pick_out, axis=1))
    return weighted_sum / (own_weight + lax.optimization_barrier(jnp.sum(pick_weight, axis=1)))[..., None]

def reference(queries, keys, values, picks, out_weight):
    owner_count = SEQUENCE_TOKENS // BLOCK_TOKENS
    heads_per_group = QUERY_HEADS // KEY_VALUE_HEADS
    score_scale = 1.0 / math.sqrt(HEAD_SIZE)
    slot_count_total = owner_count * CAP
    grouped = picks.reshape(owner_count, 2 * BLOCK_TOKENS)
    owner_ids = jnp.arange(owner_count, dtype=jnp.int32)
    matches = (grouped[:, :, None] == owner_ids[None, None, :]).astype(jnp.int32)
    pick_rank = lax.optimization_barrier(jnp.sum((jnp.cumsum(matches, axis=1) - 1) * matches, axis=2)).astype(jnp.int32)
    is_live = grouped >= 0
    slot_index = (jnp.maximum(grouped, 0) * owner_count + owner_ids[:, None]) * CAP + pick_rank
    slot_index = jnp.where(is_live, slot_index, owner_count * slot_count_total).astype(jnp.int32)
    item_index = jnp.arange(2 * SEQUENCE_TOKENS, dtype=jnp.int32)
    slot_items = jnp.zeros((owner_count * slot_count_total,), jnp.int32).at[slot_index.reshape(-1)].set(item_index, mode='drop')

    def remote_block(holding_block):
        selected_blocks = lax.dynamic_slice_in_dim(slot_items, holding_block * slot_count_total, slot_count_total)
        query_matrix = queries[selected_blocks // 2].astype(jnp.float32).reshape(slot_count_total, KEY_VALUE_HEADS, heads_per_group, HEAD_SIZE)
        key_matrix = lax.dynamic_slice_in_dim(keys, holding_block * BLOCK_TOKENS, BLOCK_TOKENS).astype(jnp.float32).reshape(BLOCK_TOKENS, KEY_VALUE_HEADS, HEAD_SIZE)
        value_matrix = lax.dynamic_slice_in_dim(values, holding_block * BLOCK_TOKENS, BLOCK_TOKENS).astype(jnp.float32).reshape(BLOCK_TOKENS, KEY_VALUE_HEADS, HEAD_SIZE)
        scores = jnp.einsum('sjgd,kjd->jgsk', query_matrix, key_matrix) * score_scale
        peak_score = lax.optimization_barrier(jnp.max(scores, axis=-1))
        weights = jnp.exp(scores - peak_score[..., None])
        totals = lax.optimization_barrier(jnp.sum(weights, axis=-1))
        rounded = lax.optimization_barrier(weights.astype(jnp.bfloat16)).astype(jnp.float32)
        mixed_rows = jnp.einsum('jgsk,kjd->sjgd', rounded, value_matrix)
        mixed_rows = mixed_rows / jnp.transpose(totals, (2, 0, 1))[..., None]
        return (mixed_rows.reshape(slot_count_total, QUERY_HEADS * HEAD_SIZE), jnp.transpose(peak_score, (2, 0, 1)).reshape(slot_count_total, QUERY_HEADS), jnp.transpose(totals, (2, 0, 1)).reshape(slot_count_total, QUERY_HEADS))
    part_out, part_peak, part_total = lax.map(remote_block, owner_ids)
    part_out = part_out.reshape(-1, QUERY_HEADS, HEAD_SIZE)
    part_peak = part_peak.reshape(-1, QUERY_HEADS)
    part_total = part_total.reshape(-1, QUERY_HEADS)

    def query_block(block_number):
        local_rows = lax.dynamic_slice_in_dim(queries, block_number * BLOCK_TOKENS, BLOCK_TOKENS).astype(jnp.float32).reshape(BLOCK_TOKENS, KEY_VALUE_HEADS, heads_per_group, HEAD_SIZE)
        key_matrix = lax.dynamic_slice_in_dim(keys, block_number * BLOCK_TOKENS, BLOCK_TOKENS).astype(jnp.float32).reshape(BLOCK_TOKENS, KEY_VALUE_HEADS, HEAD_SIZE)
        value_matrix = lax.dynamic_slice_in_dim(values, block_number * BLOCK_TOKENS, BLOCK_TOKENS).astype(jnp.float32).reshape(BLOCK_TOKENS, KEY_VALUE_HEADS, HEAD_SIZE)
        own_out, own_peak, own_total = own_partial(local_rows, key_matrix, value_matrix, 0, score_scale)
        safe_index = jnp.minimum(slot_index[block_number], owner_count * slot_count_total - 1)
        pick_out = part_out[safe_index].reshape(BLOCK_TOKENS, 2, QUERY_HEADS, HEAD_SIZE)
        pick_peak = part_peak[safe_index].reshape(BLOCK_TOKENS, 2, QUERY_HEADS)
        pick_total = part_total[safe_index].reshape(BLOCK_TOKENS, 2, QUERY_HEADS)
        live_rows = is_live[block_number].reshape(BLOCK_TOKENS, 2)
        attention = merge_parts(own_out, own_peak, own_total, pick_out, pick_peak, pick_total, live_rows)
        attention = attention.reshape(BLOCK_TOKENS, QUERY_HEADS * HEAD_SIZE).astype(jnp.bfloat16)
        return jnp.dot(attention, out_weight, preferred_element_type=jnp.float32).astype(jnp.bfloat16)
    mixed = lax.map(query_block, owner_ids)
    return mixed.reshape(SEQUENCE_TOKENS, D)
```

```python
import functools
import math

import jax
import jax.numpy as jnp
from jax import lax
from jax.experimental import pallas as pl
from jax.experimental.pallas import tpu as pltpu
from jax.sharding import PartitionSpec as P

HEAD_SIZE = 128
CAP = 6
NEG_FILL = -1e30
MESH = pl.DeviceIdType.MESH


def greet_all(owner_count):
    me = lax.axis_index("seq")
    barrier = pltpu.get_barrier_semaphore()

    def greet(i, carry):
        pl.semaphore_signal(
            barrier, inc=1, device_id={"seq": lax.rem(me + i, owner_count)}, device_id_type=MESH
        )
        return carry

    lax.fori_loop(1, owner_count, greet, 0)
    pl.semaphore_wait(barrier, owner_count - 1)


def down_kernel(owner_count, out_ref, in_ref, send_sem, recv_sem):
    me = lax.axis_index("seq")
    greet_all(owner_count)

    def copy_to(b):
        return pltpu.make_async_remote_copy(
            src_ref=out_ref.at[b],
            dst_ref=in_ref.at[me],
            send_sem=send_sem.at[b],
            recv_sem=recv_sem.at[me],
            device_id={"seq": b},
            device_id_type=MESH,
        )

    def copy_from(d):
        return pltpu.make_async_remote_copy(
            src_ref=out_ref.at[d],
            dst_ref=in_ref.at[d],
            send_sem=send_sem.at[d],
            recv_sem=recv_sem.at[d],
            device_id={"seq": d},
            device_id_type=MESH,
        )

    lax.fori_loop(0, me, lambda i, c: (copy_to(me - 1 - i).start(), c)[1], 0)
    lax.fori_loop(me + 1, owner_count, lambda d, c: (copy_from(d).wait_recv(), c)[1], 0)
    lax.fori_loop(0, me, lambda b, c: (copy_to(b).wait_send(), c)[1], 0)


def up_kernel(owner_count, out_ref, stat_out, in_ref, stat_in, send_sem, recv_sem):
    me = lax.axis_index("seq")
    greet_all(owner_count)

    def copies(peer, slot):
        return [
            pltpu.make_async_remote_copy(
                src_ref=source.at[peer],
                dst_ref=target.at[slot],
                send_sem=send_sem.at[k, peer],
                recv_sem=recv_sem.at[k, slot],
                device_id={"seq": peer},
                device_id_type=MESH,
            )
            for k, (source, target) in enumerate(((out_ref, in_ref), (stat_out, stat_in)))
        ]

    def start(d, carry):
        for copy in copies(d, me):
            copy.start()
        return carry

    def wait_recv(b, carry):
        for copy in copies(b, b):
            copy.wait_recv()
        return carry

    def wait_send(d, carry):
        for copy in copies(d, me):
            copy.wait_send()
        return carry

    lax.fori_loop(me + 1, owner_count, start, 0)
    lax.fori_loop(0, me, wait_recv, 0)
    lax.fori_loop(me + 1, owner_count, wait_send, 0)


def ring_steps(buf, axis_pos, extent, unit, to, sems):
    up_send, up_recv, down_send, down_recv = sems
    half = extent // 2

    def up(step):
        block = unit(lax.rem(axis_pos - step + 1 + extent, extent))
        return pltpu.make_async_remote_copy(
            src_ref=block, dst_ref=block, send_sem=up_send.at[step], recv_sem=up_recv.at[step],
            device_id=to(lax.rem(axis_pos + 1, extent)), device_id_type=MESH)

    def down(step):
        block = unit(lax.rem(axis_pos + step - 1, extent))
        return pltpu.make_async_remote_copy(
            src_ref=block, dst_ref=block, send_sem=down_send.at[step], recv_sem=down_recv.at[step],
            device_id=to(lax.rem(axis_pos + extent - 1, extent)), device_id_type=MESH)

    return up, down, half


def weight_kernel(w_ref, full, local_sem, send_sem, recv_sem, sib_send, sib_recv):
    me = lax.axis_index("seq")
    core = lax.rem(me, 2)
    z = lax.rem(me // 2, 8)
    y = me // 16

    def at(yy, zz, cc):
        return {"seq": (yy * 8 + zz) * 2 + cc}

    barrier = pltpu.get_barrier_semaphore()
    friends = [
        at(y, lax.rem(z + 1, 8), core),
        at(y, lax.rem(z + 7, 8), core),
        at(lax.rem(y + 1, 8), z, core),
        at(lax.rem(y + 7, 8), z, core),
        at(y, z, 1 - core),
    ]
    for friend in friends:
        pl.semaphore_signal(barrier, inc=1, device_id=friend, device_id_type=MESH)
    local = pltpu.make_async_copy(w_ref, full.at[y, z, core], local_sem)
    local.start()
    pl.semaphore_wait(barrier, 5)
    local.wait()

    def rings(phase):
        made = []
        for h in range(2):
            along_z = (h == 0) == (phase == 0)
            sems = [s.at[phase, h, i] for i in range(2) for s in (send_sem, recv_sem)]
            if along_z:
                if phase == 0:
                    unit = lambda p, h=h: full.at[y, p, core, h]
                else:
                    unit = lambda p, h=h: full.at[:, p, core, h]
                made.append(ring_steps(full, z, 8, unit, lambda p: at(y, p, core), sems))
            else:
                if phase == 0:
                    unit = lambda p, h=h: full.at[p, z, core, h]
                else:
                    unit = lambda p, h=h: full.at[p, :, core, h]
                made.append(ring_steps(full, y, 8, unit, lambda p: at(p, z, core), sems))
        return made

    def sibling(h, p):
        unit = full.at[p, :, core, h] if h == 0 else full.at[:, p, core, h]
        return pltpu.make_async_remote_copy(
            src_ref=unit, dst_ref=unit, send_sem=sib_send.at[h, p], recv_sem=sib_recv.at[h, p],
            device_id=at(y, z, 1 - core), device_id_type=MESH)

    def sibling_in(h, p):
        unit = full.at[p, :, 1 - core, h] if h == 0 else full.at[:, p, 1 - core, h]
        return pltpu.make_async_remote_copy(
            src_ref=unit, dst_ref=unit, send_sem=sib_send.at[h, p], recv_sem=sib_recv.at[h, p],
            device_id=at(y, z, 1 - core), device_id_type=MESH)

    for phase in range(2):
        made = rings(phase)
        if phase == 1:
            for h in range(2):
                sibling(h, (y, z)[h]).start()
        for step in range(1, 5):
            for up, down, _ in made:
                up(step).start()
                if step < 4:
                    down(step).start()
            for h, (up, down, _) in enumerate(made):
                pos = (y, z)[h]
                up(step).wait_recv()
                if phase == 1:
                    sibling(h, lax.rem(pos - step + 8, 8)).start()
                if step < 4:
                    down(step).wait_recv()
                    if phase == 1:
                        sibling(h, lax.rem(pos + step, 8)).start()
        for step in range(1, 5):
            for up, down, _ in made:
                up(step).wait_send()
                if step < 4:
                    down(step).wait_send()
    for h in range(2):
        for p in range(8):
            sibling_in(h, p).wait_recv()
            sibling(h, p).wait_send()


def head_kernel(a_ref, full, local_sem, send_sem, recv_sem):
    x = lax.axis_index("head")
    right, left = lax.rem(x + 1, 4), lax.rem(x + 3, 4)
    rows = a_ref.shape[0]
    barrier = pltpu.get_barrier_semaphore()
    for friend in (right, left):
        pl.semaphore_signal(barrier, inc=1, device_id={"head": friend}, device_id_type=MESH)
    local = pltpu.make_async_copy(a_ref, full.at[x], local_sem)
    local.start()
    pl.semaphore_wait(barrier, 2)

    def move(k, src, dst, to):
        return pltpu.make_async_remote_copy(
            src_ref=src, dst_ref=dst, send_sem=send_sem.at[k], recv_sem=recv_sem.at[k],
            device_id={"head": to}, device_id_type=MESH)

    first = pl.ds(0, rows // 2)
    second = pl.ds(rows // 2, rows // 2)
    out = [
        [move(0, a_ref.at[first], full.at[x, first], right), move(1, a_ref.at[second], full.at[x, second], right)],
        [move(2, a_ref.at[second], full.at[x, second], left), move(3, a_ref.at[first], full.at[x, first], left)],
    ]
    for k in range(2):
        for side in out:
            side[k].start()
    out[0][0].wait_recv()
    onward = move(4, full.at[left, first], full.at[left, first], right)
    onward.start()
    out[1][0].wait_recv()
    back = move(5, full.at[right, second], full.at[right, second], left)
    back.start()
    out[0][1].wait_recv()
    out[1][1].wait_recv()
    onward.wait_recv()
    back.wait_recv()
    for side in out:
        for copy in side:
            copy.wait_send()
    onward.wait_send()
    back.wait_send()
    local.wait()


VM = pl.BlockSpec(memory_space=pltpu.VMEM)
DMA = pltpu.SemaphoreType.DMA


def call(kernel, collective_id, out_shape, scratch, *args):
    single = not isinstance(out_shape, (tuple, list))
    return pl.pallas_call(
        kernel,
        out_shape=out_shape,
        in_specs=[VM] * len(args),
        out_specs=VM if single else [VM] * len(out_shape),
        scratch_shapes=scratch,
        compiler_params=pltpu.CompilerParams(
            collective_id=collective_id, has_side_effects=True, vmem_limit_bytes=40 << 20
        ),
    )(*args)


def own_partial(query_matrix, key_matrix, value_matrix, score_scale):
    row_count = query_matrix.shape[0]
    key_count = key_matrix.shape[0]
    scores = (
        jnp.einsum("qjgd,kjd->jgqk", query_matrix, key_matrix, preferred_element_type=jnp.float32)
        * score_scale
    )
    visible = jnp.arange(key_count)[None, :] <= jnp.arange(row_count)[:, None]
    scores = jnp.where(visible, scores, NEG_FILL)
    peak_score = jnp.max(scores, axis=-1)
    weights = jnp.where(visible, jnp.exp(scores - peak_score[..., None]), 0.0)
    totals = jnp.sum(weights, axis=-1)
    mixed_rows = jnp.einsum(
        "jgqk,kjd->qjgd",
        weights.astype(jnp.bfloat16),
        value_matrix,
        preferred_element_type=jnp.float32,
    )
    mixed_rows = mixed_rows / jnp.transpose(totals, (2, 0, 1))[..., None]
    return (
        mixed_rows.reshape(row_count, -1, HEAD_SIZE),
        jnp.transpose(peak_score, (2, 0, 1)).reshape(row_count, -1),
        jnp.transpose(totals, (2, 0, 1)).reshape(row_count, -1),
    )


def merge_parts(own_out, own_peak, own_total, pick_out, pick_peak, pick_total, live_rows):
    live_mask = live_rows[:, :, None]
    pick_peak = jnp.where(live_mask, pick_peak, own_peak[:, None, :])
    pick_out = jnp.where(live_mask[..., None], pick_out, 0.0)
    summit = jnp.maximum(own_peak, jnp.max(pick_peak, axis=1))
    own_weight = own_total * jnp.exp(own_peak - summit)
    pick_weight = jnp.where(live_mask, pick_total * jnp.exp(pick_peak - summit[:, None, :]), 0.0)
    weighted_sum = own_weight[..., None] * own_out + jnp.sum(
        pick_weight[..., None] * pick_out, axis=1
    )
    return weighted_sum / (own_weight + jnp.sum(pick_weight, axis=1))[..., None]


def on_device(queries, keys, values, picks, out_weight):
    owner_count = lax.axis_size("seq")
    block_len = queries.shape[0]
    kv_local = keys.shape[1] // HEAD_SIZE
    heads_local = queries.shape[1] // HEAD_SIZE
    heads_per_group = heads_local // kv_local
    score_scale = 1.0 / math.sqrt(HEAD_SIZE)
    slot_count_total = owner_count * CAP
    full_weight = call(
        weight_kernel, 0, jax.ShapeDtypeStruct((8, 8, 2, 2, 16, 1024), jnp.bfloat16),
        [DMA, DMA((2, 2, 2, 5)), DMA((2, 2, 2, 5)), DMA((2, 8)), DMA((2, 8))],
        out_weight.reshape(2, 16, 1024))
    flat_picks = picks.reshape(-1)
    owner_ids = jnp.arange(owner_count, dtype=jnp.int32)
    matches = (flat_picks[:, None] == owner_ids[None, :]).astype(jnp.int32)
    pick_rank = jnp.sum((jnp.cumsum(matches, axis=0) - 1) * matches, axis=1)
    is_live = flat_picks >= 0
    slot_index = jnp.where(is_live, flat_picks * CAP + pick_rank, slot_count_total)
    slot_rows = (
        jnp.zeros((slot_count_total,), jnp.int32)
        .at[slot_index]
        .set(jnp.arange(2 * block_len, dtype=jnp.int32) // 2, mode="drop")
    )
    outgoing = queries[slot_rows].reshape(owner_count, CAP * heads_local, HEAD_SIZE)
    key_heads = keys.reshape(block_len, kv_local, HEAD_SIZE)
    value_heads = values.reshape(block_len, kv_local, HEAD_SIZE)
    arrived = call(
        functools.partial(down_kernel, owner_count), 1,
        jax.ShapeDtypeStruct(outgoing.shape, jnp.bfloat16),
        [DMA((owner_count,)), DMA((owner_count,))], outgoing)
    arrived = arrived.reshape(owner_count, CAP, heads_local * HEAD_SIZE)
    live_source = jnp.arange(owner_count) > lax.axis_index("seq")
    arrived = jnp.where(live_source[:, None, None], arrived, 0)
    sources, slot_width, features = arrived.shape
    query_matrix = arrived.reshape(sources * slot_width, kv_local, heads_per_group, HEAD_SIZE)
    scores = (
        jnp.einsum("sjgd,kjd->jgsk", query_matrix, key_heads, preferred_element_type=jnp.float32)
        * score_scale
    )
    peak_score = jnp.max(scores, axis=-1)
    weights = jnp.exp(scores - peak_score[..., None])
    totals = jnp.sum(weights, axis=-1)
    mixed_rows = jnp.einsum(
        "jgsk,kjd->sjgd",
        weights.astype(jnp.bfloat16),
        value_heads,
        preferred_element_type=jnp.float32,
    )
    mixed_rows = mixed_rows / jnp.transpose(totals, (2, 0, 1))[..., None]
    part_out = mixed_rows.astype(jnp.bfloat16).reshape(sources, slot_width * heads_local, HEAD_SIZE)
    stats = jnp.concatenate(
        [
            jnp.transpose(peak_score, (2, 0, 1)).reshape(sources, slot_width * heads_local),
            jnp.transpose(totals, (2, 0, 1)).reshape(sources, slot_width * heads_local),
        ],
        axis=1,
    )
    stats = jnp.pad(stats, ((0, 0), (0, 128 - stats.shape[1])))[:, None, :]
    part_out, stats = call(
        functools.partial(up_kernel, owner_count), 2,
        [jax.ShapeDtypeStruct(part_out.shape, jnp.bfloat16), jax.ShapeDtypeStruct(stats.shape, jnp.float32)],
        [DMA((2, owner_count)), DMA((2, owner_count))], part_out, stats)
    count = slot_width * heads_local
    part_peak = stats[:, 0, :count].reshape(slot_count_total, heads_local)
    part_total = stats[:, 0, count:2 * count].reshape(slot_count_total, heads_local)
    safe_index = jnp.minimum(slot_index, slot_count_total - 1)
    pick_out = part_out.reshape(slot_count_total, heads_local, HEAD_SIZE)[safe_index].reshape(
        block_len, 2, heads_local, HEAD_SIZE
    )
    pick_peak = part_peak[safe_index].reshape(block_len, 2, heads_local)
    pick_total = part_total[safe_index].reshape(block_len, 2, heads_local)
    live_rows = is_live.reshape(block_len, 2)
    local_rows = queries.reshape(block_len, kv_local, heads_per_group, HEAD_SIZE)
    own_out, own_peak, own_total = own_partial(local_rows, key_heads, value_heads, score_scale)
    attention = merge_parts(
        own_out, own_peak, own_total, pick_out.astype(jnp.float32), pick_peak, pick_total, live_rows
    )
    attention = attention.reshape(block_len, heads_local * HEAD_SIZE).astype(jnp.bfloat16)
    every_head = call(
        head_kernel, 3, jax.ShapeDtypeStruct((4, block_len, heads_local * HEAD_SIZE), jnp.bfloat16),
        [DMA, DMA((6,)), DMA((6,))], attention)
    return jnp.einsum(
        "hti,hio->to",
        every_head,
        full_weight.reshape(4, 1024, 1024),
        preferred_element_type=jnp.float32,
    ).astype(jnp.bfloat16)


def solution(mesh):
    return jax.shard_map(
        on_device,
        mesh=mesh,
        in_specs=(
            P("seq", "head"),
            P("seq", "head"),
            P("seq", "head"),
            P("seq", None),
            P("seq", "head"),
        ),
        out_specs=P("seq", "head"),
        check_vma=False,
    )
```

```python
import functools
import math

import jax
import jax.numpy as jnp
from jax import lax
from jax.experimental import pallas as pl
from jax.experimental.pallas import tpu as pltpu
from jax.sharding import PartitionSpec as P

HEAD = 128
CAP = 6
BLOCK = 512
OWNERS = 128
GROUP = 4
KV = 2
ROWS = CAP * GROUP
SLOTS = CAP * OWNERS
BATCH = 8
MESH = pl.DeviceIdType.MESH
F32 = jnp.float32
BF16 = jnp.bfloat16
LOG2E = 1.0 / math.log(2.0)
SCALE = LOG2E / math.sqrt(HEAD)


def dot(a, b):
    return lax.dot_general(a, b, (((1,), (0,)), ((), ())), preferred_element_type=F32)


def dot_t(a, b):
    return lax.dot_general(a, b, (((1,), (1,)), ((), ())), preferred_element_type=F32)


def loop(low, high, body):
    def step(i, carry):
        body(i)
        return carry

    lax.fori_loop(low, high, step, 0)


def iota(shape, dim):
    return lax.broadcasted_iota(jnp.int32, shape, dim)


def kernel(
    q_ref, k_ref, v_ref, picks_ref, w_ref, out_ref,
    rows32, q_out, q_in, part_out, part_in, stat_out, stat_in,
    own_out, own_peak, own_total, pick_rank, choose, full, every, total,
    q_send, q_recv, p_send, p_recv, s_send, s_recv,
    w_local, w_send, w_recv, sib_send, sib_recv, x_send, x_recv,
):
    me = lax.axis_index("seq")
    x = lax.axis_index("head")
    core = lax.rem(me, 2)
    z = lax.rem(me // 2, 8)
    y = me // 16
    right, left = lax.rem(x + 1, 4), lax.rem(x + 3, 4)

    part_in[...] = jnp.zeros_like(part_in)
    stat_in[...] = jnp.zeros_like(stat_in)

    barrier = pltpu.get_barrier_semaphore()
    loop(1, OWNERS, lambda i: pl.semaphore_signal(
        barrier, inc=1, device_id={"seq": lax.rem(me + i, OWNERS)}, device_id_type=MESH))
    for friend in (right, left):
        pl.semaphore_signal(barrier, inc=1, device_id={"head": friend}, device_id_type=MESH)

    w_copy = pltpu.make_async_copy(w_ref, full.at[y, z, core], w_local)
    w_copy.start()

    picks = picks_ref[...]
    first, second = picks[:, 0:1], picks[:, 1:2]
    lanes = iota((BLOCK, OWNERS), 1)
    hit0, hit1 = first == lanes, second == lanes
    named = jnp.where(hit0 | hit1, 1.0, 0.0).astype(BF16)
    before = jnp.where(iota((BLOCK, BLOCK), 0) > iota((BLOCK, BLOCK), 1), 1.0, 0.0).astype(BF16)
    rank = dot(before, named)
    rank0 = jnp.sum(jnp.where(hit0, rank, 0.0), axis=1, keepdims=True).astype(jnp.int32)
    rank1 = jnp.sum(jnp.where(hit1, rank, 0.0), axis=1, keepdims=True).astype(jnp.int32)
    pick_rank[0] = rank0
    pick_rank[1] = rank1
    slot0 = jnp.where(first >= 0, rank0 * OWNERS + first, -1)
    slot1 = jnp.where(second >= 0, rank1 * OWNERS + second, -1)
    for r in range(CAP):
        at = iota((BLOCK, OWNERS), 1) + r * OWNERS
        choose[0:BLOCK, r * OWNERS:(r + 1) * OWNERS] = jnp.where(slot0 == at, 1.0, 0.0).astype(BF16)
        choose[BLOCK:, r * OWNERS:(r + 1) * OWNERS] = jnp.where(slot1 == at, 1.0, 0.0).astype(BF16)
    slots = jnp.where(lanes == 0, slot0, jnp.where(lanes == 1, slot1, -1)).astype(F32)
    slots = jnp.transpose(slots)
    across0, across1 = slots[0:1].astype(jnp.int32), slots[1:2].astype(jnp.int32)
    for r in range(CAP):
        at = iota((OWNERS, BLOCK), 0) + r * OWNERS
        pick = jnp.where((across0 == at) | (across1 == at), 1.0, 0.0).astype(BF16)
        for j in range(KV):
            got = dot(pick, q_ref[:, j * GROUP * HEAD:(j + 1) * GROUP * HEAD])
            for g in range(GROUP):
                rows32[j, pl.ds(GROUP * r + g, OWNERS, ROWS), :] = got[:, g * HEAD:(g + 1) * HEAD]

    def pack(j):
        def some(i):
            block = rows32[j, pl.ds(pl.multiple_of(i * 16 * ROWS, 16 * ROWS), 16 * ROWS), :]
            q_out[j, pl.ds(i * 16, 16)] = block.reshape(16, ROWS, HEAD).astype(BF16)

        loop(0, OWNERS // 16, some)

    for j in range(KV):
        pack(j)
    w_copy.wait()
    pl.semaphore_wait(barrier, OWNERS + 1)

    def move(src, dst, send_sem, recv_sem, to):
        return pltpu.make_async_remote_copy(
            src_ref=src, dst_ref=dst, send_sem=send_sem, recv_sem=recv_sem,
            device_id=to, device_id_type=MESH)

    def query(j, peer, slot):
        return move(q_out.at[j, peer], q_in.at[j, slot], q_send.at[j, peer], q_recv.at[j, slot], {"seq": peer})

    def part(j, peer, slot):
        return move(part_out.at[j, peer], part_in.at[j, slot], p_send.at[j, peer], p_recv.at[j, slot], {"seq": peer})

    def stat(j, peer, slot):
        return move(stat_out.at[j, peer], stat_in.at[j, slot], s_send.at[j, peer], s_recv.at[j, slot], {"seq": peer})

    def send_queries(j):
        loop(0, me, lambda i: query(j, me - 1 - i, me).start())

    def device(yy, zz, cc):
        return {"seq": (yy * 8 + zz) * 2 + cc}

    def w_unit(phase, h, p, c):
        if phase == 0:
            return full.at[y, p, c, h] if h == 0 else full.at[p, z, c, h]
        return full.at[p, :, c, h] if h == 0 else full.at[:, p, c, h]

    def w_move(phase, h, step, way):
        along_z = (h == 0) == (phase == 0)
        pos = z if along_z else y
        ahead = lax.rem(pos + 8 + way, 8)
        unit = w_unit(phase, h, lax.rem(pos - way * (step - 1) + 8, 8), core)
        to = device(y, ahead, core) if along_z else device(ahead, z, core)
        i = 0 if way > 0 else 1
        return move(unit, unit, w_send.at[phase, h, i, step], w_recv.at[phase, h, i, step], to)

    def sibling(h, p, c):
        unit = w_unit(1, h, p, c)
        return move(unit, unit, sib_send.at[h, p], sib_recv.at[h, p], device(y, z, 1 - core))

    def w_moves(phase, step):
        ways = (1, -1) if step < 4 else (1,)
        return [(h, way, w_move(phase, h, step, way)) for way in ways for h in range(2)]

    def w_start(phase, step):
        if phase == 1 and step == 1:
            for h in range(2):
                sibling(h, (y, z)[h], core).start()
        for _, _, copy in w_moves(phase, step):
            copy.start()

    def w_wait(phase, step):
        for h, way, copy in w_moves(phase, step):
            copy.wait_recv()
            if phase == 1:
                sibling(h, lax.rem((y, z)[h] - way * step + 8, 8), core).start()

    def w_next(phase, step):
        w_wait(phase, step)
        if step < 4:
            w_start(phase, step + 1)
        elif phase == 0:
            w_start(1, 1)

    def own(h):
        j = h // GROUP
        for part_no in range(2):
            rows = slice(part_no * 256, part_no * 256 + 256)
            keys = (part_no + 1) * 256
            s = dot_t(q_ref[rows, h * HEAD:(h + 1) * HEAD], k_ref[0:keys, j * HEAD:(j + 1) * HEAD])
            seen = iota((256, keys), 1) <= iota((256, keys), 0) + part_no * 256
            s = jnp.where(seen, s, -1e30)
            peak = jnp.max(s, axis=1, keepdims=True)
            weights = jnp.exp2((s - peak) * SCALE)
            own_peak[h, rows] = peak * SCALE
            own_total[h, rows] = jnp.sum(weights, axis=1, keepdims=True)
            own_out[rows, h * HEAD:(h + 1) * HEAD] = dot(
                weights.astype(BF16), v_ref[0:keys, j * HEAD:(j + 1) * HEAD])

    def remote(j, n):
        base = n * BATCH
        low = jnp.maximum(base, me + 1)
        loop(low, base + BATCH, lambda d: query(j, d, d).wait_recv())
        batch = pl.ds(base, BATCH)
        rows = q_in[j, batch].astype(F32).reshape(BATCH * ROWS, HEAD).astype(BF16)
        s = dot_t(rows, k_ref[:, j * HEAD:(j + 1) * HEAD])
        peak = jnp.max(s, axis=1, keepdims=True)
        weights = jnp.exp2((s - peak) * SCALE)
        mass = jnp.sum(weights, axis=1, keepdims=True)
        mixed = dot(weights.astype(BF16), v_ref[:, j * HEAD:(j + 1) * HEAD]) * (1.0 / mass)
        part_out[j, batch] = mixed.reshape(BATCH, ROWS, HEAD).astype(BF16)
        level = peak * SCALE + jnp.log(mass) * LOG2E
        level = jnp.broadcast_to(level, (BATCH * ROWS, HEAD)).reshape(BATCH, ROWS, HEAD)
        diagonal = iota(level.shape, 1) == iota(level.shape, 2)
        stat_out[j, batch] = jnp.sum(jnp.where(diagonal, level, 0.0), axis=1, keepdims=True)

        def answer(d):
            part(j, d, me).start()
            stat(j, d, me).start()

        loop(low, base + BATCH, answer)

    low_batch = (me + 1) // BATCH
    batches = OWNERS // BATCH - low_batch

    def remote_some(j, i, count):
        loop(low_batch + batches * i // count, low_batch + batches * (i + 1) // count, lambda n: remote(j, n))

    def combine(j):
        def arrived(b):
            part(j, b, b).wait_recv()
            stat(j, b, b).wait_recv()

        loop(0, me, arrived)

        def widen(i):
            rows32[j, pl.ds(pl.multiple_of(i * 16 * ROWS, 16 * ROWS), 16 * ROWS), :] = (
                part_in[j, pl.ds(i * 16, 16)].astype(F32).reshape(16 * ROWS, HEAD))

        loop(0, OWNERS // 16, widen)
        picks = picks_ref[...]
        lane = iota((BLOCK, OWNERS), 1)
        levels = jnp.sum(stat_in[j], axis=1)
        high = levels.astype(BF16)
        rest = levels - high.astype(F32)
        mid = rest.astype(BF16)
        low = (rest - mid.astype(F32)).astype(BF16)
        found = []
        for c in range(2):
            hit = jnp.where(picks[:, c:c + 1] == lane, 1.0, 0.0).astype(BF16)
            found.append(dot(hit, high) + dot(hit, mid) + dot(hit, low))
        for g in range(GROUP):
            h = j * GROUP + g
            source = jnp.concatenate(
                [rows32[j, pl.ds(GROUP * r + g, OWNERS, ROWS), :].astype(BF16) for r in range(CAP)], axis=0)
            got = dot(choose[...], source)
            peak, mass = own_peak[h], own_total[h]
            level, live = [], []
            for c in range(2):
                here = lane == pick_rank[c] * GROUP + g
                live.append(picks[:, c:c + 1] >= 0)
                level.append(jnp.sum(jnp.where(here, found[c], 0.0), axis=1, keepdims=True))
            top = peak
            for c in range(2):
                top = jnp.maximum(top, jnp.where(live[c], level[c], peak))
            own_share = jnp.exp2(peak - top)
            share = [jnp.where(live[c], jnp.exp2(level[c] - top), 0.0) for c in range(2)]
            norm = 1.0 / (own_share * mass + share[0] + share[1])
            mixed = own_out[:, h * HEAD:(h + 1) * HEAD] * (own_share * norm)
            mixed += got[0:BLOCK] * (share[0] * norm) + got[BLOCK:] * (share[1] * norm)
            every[x, j, :, g * HEAD:(g + 1) * HEAD] = mixed.astype(BF16)

    upper, lower = pl.ds(0, BLOCK // 2), pl.ds(BLOCK // 2, BLOCK // 2)

    def x_move(j, i, owner, rows, to):
        unit = every.at[owner, j, rows]
        return move(unit, unit, x_send.at[j, i], x_recv.at[j, i], {"head": to})

    def x_copies(j):
        return [
            x_move(j, 0, x, upper, right), x_move(j, 1, x, lower, left),
            x_move(j, 2, x, lower, right), x_move(j, 3, x, upper, left),
        ]

    def x_onward(j):
        return [x_move(j, 4, left, upper, right), x_move(j, 5, right, lower, left)]

    def x_start(j):
        for copy in x_copies(j):
            copy.start()

    def x_forward(j):
        copies, onward = x_copies(j), x_onward(j)
        for i in range(2):
            copies[i].wait_recv()
            onward[i].start()

    def project(owner, j, first_term):
        a = every[owner, j]
        for n in range(4):
            cols = slice(n * 256, n * 256 + 256)
            w = full[2 * owner + j, :, :, :, :, cols].reshape(BLOCK, 256)
            term = dot(a, w)
            total[:, cols] = term if first_term else total[:, cols] + term

    send_queries(0)
    w_start(0, 1)
    own(0)
    send_queries(1)
    for h in range(1, KV * GROUP):
        own(h)
        if h % 2 == 1:
            w_next(0, h // 2 + 1)
    remote_some(0, 0, 2)
    w_next(1, 1)
    remote_some(0, 1, 2)
    w_next(1, 2)
    remote_some(1, 0, 2)
    combine(0)
    x_start(0)
    w_next(1, 3)
    remote_some(1, 1, 2)
    x_forward(0)
    w_wait(1, 4)
    combine(1)
    x_start(1)

    def w_sent(phase):
        for step in range(1, 5):
            for _, _, copy in w_moves(phase, step):
                copy.wait_send()

    for phase in range(2):
        w_sent(phase)
    for h in range(2):
        for p in range(8):
            sibling(h, p, 1 - core).wait_recv()
            sibling(h, p, core).wait_send()
    for copy in x_copies(0)[2:] + x_onward(0):
        copy.wait_recv()
    project(x, 0, True)
    project(left, 0, False)
    project(right, 0, False)
    x_forward(1)
    project(lax.rem(x + 2, 4), 0, False)
    project(x, 1, False)

    def sent_queries(b):
        for j in range(KV):
            query(j, b, me).wait_send()

    def sent_parts(d):
        for j in range(KV):
            part(j, d, me).wait_send()
            stat(j, d, me).wait_send()

    loop(0, me, sent_queries)
    loop(me + 1, OWNERS, sent_parts)
    for copy in x_copies(1)[2:]:
        copy.wait_recv()
    project(left, 1, False)
    project(right, 1, False)
    for copy in x_onward(1):
        copy.wait_recv()
    project(lax.rem(x + 2, 4), 1, False)
    out_ref[...] = total[...].astype(BF16)
    for j in range(KV):
        for copy in x_copies(j) + x_onward(j):
            copy.wait_send()


def on_device(queries, keys, values, picks, out_weight):
    vmem, dma = pltpu.VMEM, pltpu.SemaphoreType.DMA
    features = out_weight.shape[1]
    return pl.pallas_call(
        kernel,
        out_shape=jax.ShapeDtypeStruct((BLOCK, features), BF16),
        in_specs=[pl.BlockSpec(memory_space=vmem)] * 5,
        out_specs=pl.BlockSpec(memory_space=vmem),
        scratch_shapes=[
            vmem((KV, OWNERS * ROWS, HEAD), F32),
            vmem((KV, OWNERS, ROWS, HEAD), BF16),
            vmem((KV, OWNERS, ROWS, HEAD), BF16),
            vmem((KV, OWNERS, ROWS, HEAD), BF16),
            vmem((KV, OWNERS, ROWS, HEAD), BF16),
            vmem((KV, OWNERS, 1, HEAD), F32),
            vmem((KV, OWNERS, 1, HEAD), F32),
            vmem((BLOCK, KV * GROUP * HEAD), F32),
            vmem((KV * GROUP, BLOCK, 1), F32),
            vmem((KV * GROUP, BLOCK, 1), F32),
            vmem((2, BLOCK, 1), jnp.int32),
            vmem((2 * BLOCK, SLOTS), BF16),
            vmem((8, 8, 2, 2, 16, features), BF16),
            vmem((4, KV, BLOCK, GROUP * HEAD), BF16),
            vmem((BLOCK, features), F32),
            dma((KV, OWNERS)), dma((KV, OWNERS)),
            dma((KV, OWNERS)), dma((KV, OWNERS)),
            dma((KV, OWNERS)), dma((KV, OWNERS)),
            dma, dma((2, 2, 2, 5)), dma((2, 2, 2, 5)), dma((2, 8)), dma((2, 8)),
            dma((KV, 6)), dma((KV, 6)),
        ],
        compiler_params=pltpu.CompilerParams(
            collective_id=0, has_side_effects=True, vmem_limit_bytes=58 << 20
        ),
        cost_estimate=pl.CostEstimate(flops=7 << 30, bytes_accessed=4 << 20, transcendentals=5 << 20),
    )(queries, keys, values, picks, out_weight.reshape(2, 16, features))


def solution(mesh):
    return jax.shard_map(
        on_device,
        mesh=mesh,
        in_specs=(
            P("seq", "head"),
            P("seq", "head"),
            P("seq", "head"),
            P("seq", None),
            P("seq", "head"),
        ),
        out_specs=P("seq", "head"),
        check_vma=False,
    )
```

```python
import functools
import math

import jax
import jax.numpy as jnp
from jax import lax
from jax.experimental import pallas as pl
from jax.experimental.pallas import tpu as pltpu
from jax.sharding import PartitionSpec as P

HEAD = 128
CAP = 6
BLOCK = 512
OWNERS = 128
GROUP = 4
KV = 2
ROWS = CAP * GROUP
SLOTS = CAP * OWNERS
BATCH = 8
STRIDE = OWNERS // BATCH
MESH = pl.DeviceIdType.MESH
F32 = jnp.float32
BF16 = jnp.bfloat16
LOG2E = 1.0 / math.log(2.0)
SCALE = LOG2E / math.sqrt(HEAD)


def dot(a, b):
    return lax.dot_general(a, b, (((1,), (0,)), ((), ())), preferred_element_type=F32)


def dot_t(a, b):
    return lax.dot_general(a, b, (((1,), (1,)), ((), ())), preferred_element_type=F32)


def loop(low, high, body):
    def step(i, carry):
        body(i)
        return carry

    lax.fori_loop(low, high, step, 0)


def iota(shape, dim):
    return lax.broadcasted_iota(jnp.int32, shape, dim)


def kernel(
    q_ref, k_ref, v_ref, picks_ref, w_ref, out_ref,
    rows32, q_out, q_in, part_out, part_in, stat_out, stat_in,
    own_out, own_peak, own_total, choose, hits, ranked, dead, full, every, total,
    q_send, q_recv, p_send, p_recv, s_send, s_recv,
    w_local, w_send, w_recv, sib_send, sib_recv, x_send, x_recv,
):
    me = lax.axis_index("seq")
    x = lax.axis_index("head")
    core = lax.rem(me, 2)
    z = lax.rem(me // 2, 8)
    y = me // 16
    right, left = lax.rem(x + 1, 4), lax.rem(x + 3, 4)

    barrier = pltpu.get_barrier_semaphore()
    loop(1, OWNERS, lambda i: pl.semaphore_signal(
        barrier, inc=1, device_id={"seq": lax.rem(me + i, OWNERS)}, device_id_type=MESH))
    for friend in (right, left):
        pl.semaphore_signal(barrier, inc=1, device_id={"head": friend}, device_id_type=MESH)

    w_copy = pltpu.make_async_copy(w_ref, full.at[y, z, core], w_local)
    w_copy.start()

    def away(p):
        return STRIDE * (p % BATCH) + p // BATCH

    def place_of(block):
        return (me - block) % STRIDE * BATCH + (me - block) // STRIDE

    first, second = picks_ref[0:1, :], picks_ref[1:2, :]
    places = iota((OWNERS, BLOCK), 0)
    owners = me - away(places)
    owners = jnp.where(owners < 0, -2, owners)
    hit0, hit1 = first == owners, second == owners
    named = jnp.where(hit0 | hit1, 1.0, 0.0).astype(BF16)
    before = jnp.where(iota((BLOCK, BLOCK), 0) < iota((BLOCK, BLOCK), 1), 1.0, 0.0).astype(BF16)
    rank = dot(named, before)
    rank0 = jnp.sum(jnp.where(hit0, rank, 0.0), axis=0, keepdims=True)
    rank1 = jnp.sum(jnp.where(hit1, rank, 0.0), axis=0, keepdims=True)
    slot0 = jnp.where(first >= 0, rank0.astype(jnp.int32) * OWNERS + place_of(first), -1)
    slot1 = jnp.where(second >= 0, rank1.astype(jnp.int32) * OWNERS + place_of(second), -1)

    def gather(j):
        for r in range(CAP):
            at = places + r * OWNERS
            pick = jnp.where((slot0 == at) | (slot1 == at), 1.0, 0.0).astype(BF16)
            got = dot(pick, q_ref[:, j * GROUP * HEAD:(j + 1) * GROUP * HEAD])
            for g in range(GROUP):
                rows32[j, pl.ds(GROUP * r + g, OWNERS, ROWS), :] = got[:, g * HEAD:(g + 1) * HEAD]

        def pack(i):
            block = rows32[j, pl.ds(pl.multiple_of(i * 16 * ROWS, 16 * ROWS), 16 * ROWS), :]
            q_out[j, pl.ds(i * 16, 16)] = block.reshape(16, ROWS, HEAD).astype(BF16)

        loop(0, OWNERS // 16, pack)

    def tables():
        line = iota((OWNERS, BLOCK), 0)
        flat = jnp.where(line == 0, first.astype(F32), jnp.where(line == 1, second.astype(F32),
               jnp.where(line == 2, rank0, jnp.where(line == 3, rank1, 0.0))))
        columns = jnp.transpose(flat)
        lane = iota((BLOCK, OWNERS), 1)
        for c in range(2):
            rows = slice(c * BLOCK, (c + 1) * BLOCK)
            name = columns[:, c:c + 1].astype(jnp.int32)
            rank = columns[:, c + 2:c + 3].astype(jnp.int32)
            place = jnp.where(name >= 0, place_of(name), -1)
            slot = jnp.where(name >= 0, rank * OWNERS + place, -1)
            for r in range(CAP):
                choose[rows, r * OWNERS:(r + 1) * OWNERS] = jnp.where(slot == lane + r * OWNERS, 1.0, 0.0).astype(BF16)
            hits[rows] = jnp.where(place == lane, 1.0, 0.0).astype(BF16)
            ranked[rows] = jnp.where(rank == lane // GROUP, 1.0, 0.0)
            dead[rows] = jnp.where(jnp.broadcast_to(name, (BLOCK, 2 * HEAD)) >= 0, 0.0, -1e30)

    def move(src, dst, send_sem, recv_sem, to):
        return pltpu.make_async_remote_copy(
            src_ref=src, dst_ref=dst, send_sem=send_sem, recv_sem=recv_sem,
            device_id=to, device_id_type=MESH)

    def sender(out, into, send, recv, way):
        def copy(j, p):
            return move(out.at[j, p], into.at[j, p], send.at[j, p // BATCH], recv.at[j, p // BATCH],
                        {"seq": me + way * away(p)})
        return copy

    def waiter(out, into, send, recv):
        def wait(j, n, low, high, sent):
            for count in range(1, BATCH + 1):
                @pl.when(high - low == count)
                def _():
                    some = pl.ds(low, count)
                    copy = move(out.at[j, some], into.at[j, some], send.at[j, n], recv.at[j, n],
                                {"seq": lax.rem(me + 1, OWNERS)})
                    if sent:
                        copy.wait_send()
                    else:
                        copy.wait_recv()
        return wait

    query_sems = (q_out, q_in, q_send, q_recv)
    part_sems = (part_out, part_in, p_send, p_recv)
    stat_sems = (stat_out, stat_in, s_send, s_recv)
    query, query_wait = sender(*query_sems, -1), waiter(*query_sems)
    part, part_wait = sender(*part_sems, 1), waiter(*part_sems)
    stat, stat_wait = sender(*stat_sems, 1), waiter(*stat_sems)

    groups = OWNERS // BATCH

    def live(n, devices):
        return n * BATCH + jnp.where(n == 0, 1, 0), n * BATCH + (devices - n + STRIDE) // STRIDE

    def for_earlier(body):
        loop(0, groups, lambda n: body(n, *live(n, me)))

    def for_later(body):
        loop(0, groups, lambda n: body(n, *live(n, OWNERS - 1 - me)))

    def send_queries(j):
        for_earlier(lambda n, low, high: loop(low, high, lambda p: query(j, p).start()))

    def device(yy, zz, cc):
        return {"seq": (yy * 8 + zz) * 2 + cc}

    def w_unit(phase, h, p, c):
        if phase == 0:
            return full.at[y, p, c, h] if h == 0 else full.at[p, z, c, h]
        return full.at[p, :, c, h] if h == 0 else full.at[:, p, c, h]

    def w_move(phase, h, step, way):
        along_z = (h == 0) == (phase == 0)
        pos = z if along_z else y
        ahead = lax.rem(pos + 8 + way, 8)
        unit = w_unit(phase, h, lax.rem(pos - way * (step - 1) + 8, 8), core)
        to = device(y, ahead, core) if along_z else device(ahead, z, core)
        i = 0 if way > 0 else 1
        return move(unit, unit, w_send.at[phase, h, i, step - 1], w_recv.at[phase, h, i, step - 1], to)

    def sibling(h, p, c):
        unit = w_unit(1, h, p, c)
        return move(unit, unit, sib_send.at[h, p], sib_recv.at[h, p], device(y, z, 1 - core))

    def w_moves(phase, step):
        ways = (1, -1) if step < 4 else (1,)
        return [(h, way, w_move(phase, h, step, way)) for way in ways for h in range(2)]

    def w_start(phase, step):
        if phase == 1 and step == 1:
            for h in range(2):
                sibling(h, (y, z)[h], core).start()
        for _, _, copy in w_moves(phase, step):
            copy.start()

    def w_wait(phase, step):
        for h, way, copy in w_moves(phase, step):
            copy.wait_recv()
            if phase == 1:
                sibling(h, lax.rem((y, z)[h] - way * step + 8, 8), core).start()

    def w_next(phase, step):
        w_wait(phase, step)
        if step < 4:
            w_start(phase, step + 1)
        elif phase == 0:
            w_start(1, 1)

    def own(h):
        j = h // GROUP
        cols = slice(h * HEAD, (h + 1) * HEAD)
        for part_no in range(2):
            rows = slice(part_no * 256, part_no * 256 + 256)
            keys = (part_no + 1) * 256
            s = dot_t(q_ref[rows, cols], k_ref[0:keys, j * HEAD:(j + 1) * HEAD])
            seen = iota((256, keys), 1) <= iota((256, keys), 0) + part_no * 256
            s = jnp.where(seen, s, -1e30)
            peak = jnp.max(s, axis=1, keepdims=True)
            weights = jnp.exp2((s - peak) * SCALE)
            own_peak[rows, cols] = jnp.broadcast_to(peak * SCALE, (256, HEAD))
            own_total[rows, cols] = jnp.broadcast_to(jnp.sum(weights, axis=1, keepdims=True), (256, HEAD))
            own_out[rows, cols] = dot(weights.astype(BF16), v_ref[0:keys, j * HEAD:(j + 1) * HEAD])

    def remote(j, n):
        base = n * BATCH
        low, high = live(n, OWNERS - 1 - me)
        query_wait(j, n, low, high, False)
        batch = pl.ds(base, BATCH)
        rows = q_in[j, batch].astype(F32).reshape(BATCH * ROWS, HEAD).astype(BF16)
        s = dot_t(rows, k_ref[:, j * HEAD:(j + 1) * HEAD])
        peak = jnp.max(s, axis=1, keepdims=True)
        weights = jnp.exp2((s - peak) * SCALE)
        mass = jnp.sum(weights, axis=1, keepdims=True)
        mixed = dot(weights.astype(BF16), v_ref[:, j * HEAD:(j + 1) * HEAD]) * (1.0 / mass)
        part_out[j, batch] = mixed.reshape(BATCH, ROWS, HEAD).astype(BF16)
        level = peak * SCALE + jnp.log(mass) * LOG2E
        level = jnp.broadcast_to(level, (BATCH * ROWS, HEAD)).reshape(BATCH, ROWS, HEAD)
        diagonal = iota(level.shape, 1) == iota(level.shape, 2)
        stat_out[j, batch] = jnp.sum(jnp.where(diagonal, level, 0.0), axis=1, keepdims=True)

        def answer(d):
            part(j, d).start()
            stat(j, d).start()

        loop(low, high, answer)

    def remote_some(j, i, count):
        loop(groups * i // count, groups * (i + 1) // count, lambda n: remote(j, n))

    def combine(j):
        def arrived(n, low, high):
            part_wait(j, n, low, high, False)
            stat_wait(j, n, low, high, False)

        for_earlier(arrived)

        def widen(i):
            block = part_in[j, pl.ds(i * 16, 16)].astype(F32)
            gap = away(iota(block.shape, 0) + i * 16)
            block = jnp.where((gap > 0) & (gap <= me), block, 0.0)
            rows32[j, pl.ds(pl.multiple_of(i * 16 * ROWS, 16 * ROWS), 16 * ROWS), :] = block.reshape(16 * ROWS, HEAD)

        loop(0, OWNERS // 16, widen)
        levels = jnp.sum(stat_in[j], axis=1)
        gap = away(iota(levels.shape, 0))
        levels = jnp.where((gap > 0) & (gap <= me), levels, 0.0)
        high = levels.astype(BF16)
        rest = levels - high.astype(F32)
        mid = rest.astype(BF16)
        low = (rest - mid.astype(F32)).astype(BF16)
        found = [(dot(hits[...], piece) * ranked[...]).astype(BF16) for piece in (high, mid, low)]
        for pair in range(GROUP // 2):
            lane, head = iota((HEAD, 2 * HEAD), 0), iota((HEAD, 2 * HEAD), 1) // HEAD + 2 * pair
            spread = jnp.where((lane % GROUP == head) & (lane < ROWS), 1.0, 0.0).astype(BF16)
            source = jnp.concatenate([jnp.concatenate(
                [rows32[j, pl.ds(GROUP * r + 2 * pair + i, OWNERS, ROWS), :].astype(BF16) for i in range(2)],
                axis=1) for r in range(CAP)], axis=0)
            cols = slice((j * GROUP + 2 * pair) * HEAD, (j * GROUP + 2 * pair + 2) * HEAD)
            for half in range(2):
                rows = slice(half * 256, half * 256 + 256)
                got, level = [], []
                for c in range(2):
                    some = slice(c * BLOCK + half * 256, c * BLOCK + half * 256 + 256)
                    got.append(dot(choose[some], source))
                    level.append(sum(dot(piece[some], spread) for piece in found) + dead[some])
                peak = own_peak[rows, cols]
                top = jnp.maximum(peak, jnp.maximum(level[0], level[1]))
                own_share = jnp.exp2(peak - top)
                share = [jnp.exp2(level[c] - top) for c in range(2)]
                norm = 1.0 / (own_share * own_total[rows, cols] + share[0] + share[1])
                mixed = own_out[rows, cols] * own_share + got[0] * share[0] + got[1] * share[1]
                every[x, j, rows, 2 * pair * HEAD:(2 * pair + 2) * HEAD] = (mixed * norm).astype(BF16)

    upper, lower = pl.ds(0, BLOCK // 2), pl.ds(BLOCK // 2, BLOCK // 2)

    def x_move(j, i, owner, rows, to):
        unit = every.at[owner, j, rows]
        return move(unit, unit, x_send.at[j, i], x_recv.at[j, i], {"head": to})

    def x_copies(j):
        return [
            x_move(j, 0, x, upper, right), x_move(j, 1, x, lower, left),
            x_move(j, 2, x, lower, right), x_move(j, 3, x, upper, left),
        ]

    def x_onward(j):
        return [x_move(j, 4, left, upper, right), x_move(j, 5, right, lower, left)]

    def x_start(j):
        for copy in x_copies(j):
            copy.start()

    def x_forward(j):
        copies, onward = x_copies(j), x_onward(j)
        for i in range(2):
            copies[i].wait_recv()
            onward[i].start()

    def project(owner, j, first_term):
        a = every[owner, j]
        for n in range(4):
            cols = slice(n * 256, n * 256 + 256)
            w = full[2 * owner + j, :, :, :, :, cols].reshape(BLOCK, 256)
            term = dot(a, w)
            total[:, cols] = term if first_term else total[:, cols] + term

    def w_finish():
        for phase in range(2):
            for step in range(1, 5):
                for _, _, copy in w_moves(phase, step):
                    copy.wait_send()
        for h in range(2):
            for p in range(8):
                sibling(h, p, 1 - core).wait_recv()
                sibling(h, p, core).wait_send()

    def all_sent():
        def queries_sent(n, low, high):
            for j in range(KV):
                query_wait(j, n, low, high, True)

        def parts_sent(n, low, high):
            for j in range(KV):
                part_wait(j, n, low, high, True)
                stat_wait(j, n, low, high, True)

        for_earlier(queries_sent)
        for_later(parts_sent)

    gather(0)
    w_copy.wait()
    pl.semaphore_wait(barrier, OWNERS + 1)
    send_queries(0)
    w_start(0, 1)
    gather(1)
    send_queries(1)
    w_next(0, 1)
    tables()
    w_next(0, 2)
    for h in range(KV * GROUP):
        own(h)
        if h in (1, 4):
            w_next(0, 3 if h == 1 else 4)
    remote_some(0, 0, 1)
    w_next(1, 1)
    remote_some(1, 0, 1)
    w_next(1, 2)
    combine(0)
    x_start(0)
    w_next(1, 3)
    x_forward(0)
    combine(1)
    x_start(1)
    w_wait(1, 4)
    w_finish()
    for copy in x_copies(0)[2:] + x_onward(0):
        copy.wait_recv()
    project(x, 0, True)
    project(left, 0, False)
    project(right, 0, False)
    x_forward(1)
    project(lax.rem(x + 2, 4), 0, False)
    project(x, 1, False)
    all_sent()
    for copy in x_copies(1)[2:]:
        copy.wait_recv()
    project(left, 1, False)
    project(right, 1, False)
    for copy in x_onward(1):
        copy.wait_recv()
    project(lax.rem(x + 2, 4), 1, False)
    out_ref[...] = total[...].astype(BF16)
    for j in range(KV):
        for copy in x_copies(j) + x_onward(j):
            copy.wait_send()


def on_device(queries, keys, values, picks, out_weight):
    vmem, dma = pltpu.VMEM, pltpu.SemaphoreType.DMA
    features = out_weight.shape[1]
    return pl.pallas_call(
        kernel,
        out_shape=jax.ShapeDtypeStruct((BLOCK, features), BF16),
        in_specs=[pl.BlockSpec(memory_space=vmem)] * 5,
        out_specs=pl.BlockSpec(memory_space=vmem),
        scratch_shapes=[
            vmem((KV, OWNERS * ROWS, HEAD), F32),
            vmem((KV, OWNERS, ROWS, HEAD), BF16),
            vmem((KV, OWNERS, ROWS, HEAD), BF16),
            vmem((KV, OWNERS, ROWS, HEAD), BF16),
            vmem((KV, OWNERS, ROWS, HEAD), BF16),
            vmem((KV, OWNERS, 1, HEAD), F32),
            vmem((KV, OWNERS, 1, HEAD), F32),
            vmem((BLOCK, KV * GROUP * HEAD), F32),
            vmem((BLOCK, KV * GROUP * HEAD), F32),
            vmem((BLOCK, KV * GROUP * HEAD), F32),
            vmem((2 * BLOCK, SLOTS), BF16),
            vmem((2 * BLOCK, OWNERS), BF16),
            vmem((2 * BLOCK, OWNERS), F32),
            vmem((2 * BLOCK, 2 * HEAD), F32),
            vmem((8, 8, 2, 2, 16, features), BF16),
            vmem((4, KV, BLOCK, GROUP * HEAD), BF16),
            vmem((BLOCK, features), F32),
            dma((KV, OWNERS // BATCH)), dma((KV, OWNERS // BATCH)),
            dma((KV, OWNERS // BATCH)), dma((KV, OWNERS // BATCH)),
            dma((KV, OWNERS // BATCH)), dma((KV, OWNERS // BATCH)),
            dma, dma((2, 2, 2, 4)), dma((2, 2, 2, 4)), dma((2, 8)), dma((2, 8)),
            dma((KV, 6)), dma((KV, 6)),
        ],
        compiler_params=pltpu.CompilerParams(
            collective_id=0, has_side_effects=True, vmem_limit_bytes=58 << 20
        ),
        cost_estimate=pl.CostEstimate(flops=7 << 30, bytes_accessed=4 << 20, transcendentals=5 << 20),
    )(queries, keys, values, picks.T, out_weight.reshape(2, 16, features))


def solution(mesh):
    return jax.shard_map(
        on_device,
        mesh=mesh,
        in_specs=(
            P("seq", "head"),
            P("seq", "head"),
            P("seq", "head"),
            P("seq", None),
            P("seq", "head"),
        ),
        out_specs=P("seq", "head"),
        check_vma=False,
    )
```

```python
import functools
import math

import jax
import jax.numpy as jnp
from jax import lax
from jax.experimental import pallas as pl
from jax.experimental.pallas import tpu as pltpu
from jax.sharding import PartitionSpec as P

HEAD = 128
CAP = 6
BLOCK = 512
OWNERS = 128
GROUP = 4
KV = 2
ROWS = CAP * GROUP
SLOTS = CAP * OWNERS
BATCH = 8
STRIDE = OWNERS // BATCH
MESH = pl.DeviceIdType.MESH
F32 = jnp.float32
BF16 = jnp.bfloat16
LOG2E = 1.0 / math.log(2.0)
SCALE = LOG2E / math.sqrt(HEAD)


def dot(a, b):
    return lax.dot_general(a, b, (((1,), (0,)), ((), ())), preferred_element_type=F32)


def dot_t(a, b):
    return lax.dot_general(a, b, (((1,), (1,)), ((), ())), preferred_element_type=F32)


def loop(low, high, body):
    def step(i, carry):
        body(i)
        return carry

    lax.fori_loop(low, high, step, 0)


def iota(shape, dim):
    return lax.broadcasted_iota(jnp.int32, shape, dim)


def kernel(
    q_ref, k_ref, v_ref, picks_ref, w_ref, out_ref,
    rows32, q_out, q_in, part_out, part_in, stat_out, stat_in,
    own_out, own_peak, own_total, choose, hits, ranked, dead, full, every, total,
    q_send, q_recv, p_send, p_recv, s_send, s_recv,
    w_local, w_send, w_recv, sib_send, sib_recv, x_send, x_recv,
):
    me = lax.axis_index("seq")
    x = lax.axis_index("head")
    core = lax.rem(me, 2)
    z = lax.rem(me // 2, 8)
    y = me // 16
    right, left = lax.rem(x + 1, 4), lax.rem(x + 3, 4)

    barrier = pltpu.get_barrier_semaphore()
    loop(1, OWNERS, lambda i: pl.semaphore_signal(
        barrier, inc=1, device_id={"seq": lax.rem(me + i, OWNERS)}, device_id_type=MESH))
    for friend in (right, left):
        pl.semaphore_signal(barrier, inc=1, device_id={"head": friend}, device_id_type=MESH)

    w_copy = pltpu.make_async_copy(w_ref, full.at[y, z, core], w_local)
    w_copy.start()

    def away(p):
        return STRIDE * (p % BATCH) + p // BATCH

    def place_of(block):
        return (me - block) % STRIDE * BATCH + (me - block) // STRIDE

    first, second = picks_ref[0:1, :], picks_ref[1:2, :]
    places = iota((OWNERS, BLOCK), 0)
    owners = me - away(places)
    owners = jnp.where(owners < 0, -2, owners)
    hit0, hit1 = first == owners, second == owners
    named = jnp.where(hit0 | hit1, 1.0, 0.0).astype(BF16)
    before = jnp.where(iota((BLOCK, BLOCK), 0) < iota((BLOCK, BLOCK), 1), 1.0, 0.0).astype(BF16)
    rank = dot(named, before)
    rank0 = jnp.sum(jnp.where(hit0, rank, 0.0), axis=0, keepdims=True)
    rank1 = jnp.sum(jnp.where(hit1, rank, 0.0), axis=0, keepdims=True)
    slot0 = jnp.where(first >= 0, rank0.astype(jnp.int32) * OWNERS + place_of(first), -1)
    slot1 = jnp.where(second >= 0, rank1.astype(jnp.int32) * OWNERS + place_of(second), -1)

    def gather(j):
        for r in range(CAP):
            at = places + r * OWNERS
            pick = jnp.where((slot0 == at) | (slot1 == at), 1.0, 0.0).astype(BF16)
            got = dot(pick, q_ref[:, j * GROUP * HEAD:(j + 1) * GROUP * HEAD])
            for g in range(GROUP):
                rows32[j, pl.ds(GROUP * r + g, OWNERS, ROWS), :] = got[:, g * HEAD:(g + 1) * HEAD]

        def pack(i):
            block = rows32[j, pl.ds(pl.multiple_of(i * 16 * ROWS, 16 * ROWS), 16 * ROWS), :]
            q_out[j, pl.ds(i * 16, 16)] = block.reshape(16, ROWS, HEAD).astype(BF16)

        loop(0, OWNERS // 16, pack)

    def tables():
        line = iota((OWNERS, BLOCK), 0)
        flat = jnp.where(line == 0, first.astype(F32), jnp.where(line == 1, second.astype(F32),
               jnp.where(line == 2, rank0, jnp.where(line == 3, rank1, 0.0))))
        columns = jnp.transpose(flat)
        lane = iota((BLOCK, OWNERS), 1)
        for c in range(2):
            rows = slice(c * BLOCK, (c + 1) * BLOCK)
            name = columns[:, c:c + 1].astype(jnp.int32)
            rank = columns[:, c + 2:c + 3].astype(jnp.int32)
            place = jnp.where(name >= 0, place_of(name), -1)
            slot = jnp.where(name >= 0, rank * OWNERS + place, -1)
            for r in range(CAP):
                choose[rows, r * OWNERS:(r + 1) * OWNERS] = jnp.where(slot == lane + r * OWNERS, 1.0, 0.0).astype(BF16)
            hits[rows] = jnp.where(place == lane, 1.0, 0.0).astype(BF16)
            ranked[rows] = jnp.where(rank == lane // GROUP, 1.0, 0.0)
            dead[rows] = jnp.where(jnp.broadcast_to(name, (BLOCK, 2 * HEAD)) >= 0, 0.0, -1e30)

    def move(src, dst, send_sem, recv_sem, to):
        return pltpu.make_async_remote_copy(
            src_ref=src, dst_ref=dst, send_sem=send_sem, recv_sem=recv_sem,
            device_id=to, device_id_type=MESH)

    def sender(out, into, send, recv, way):
        def copy(j, p):
            return move(out.at[j, p], into.at[j, p], send.at[j, p // BATCH], recv.at[j, p // BATCH],
                        {"seq": me + way * away(p)})
        return copy

    def waiter(out, into, send, recv):
        def wait(j, n, low, high, sent):
            for count in range(1, BATCH + 1):
                @pl.when(high - low == count)
                def _():
                    some = pl.ds(low, count)
                    copy = move(out.at[j, some], into.at[j, some], send.at[j, n], recv.at[j, n],
                                {"seq": lax.rem(me + 1, OWNERS)})
                    if sent:
                        copy.wait_send()
                    else:
                        copy.wait_recv()
        return wait

    query_sems = (q_out, q_in, q_send, q_recv)
    part_sems = (part_out, part_in, p_send, p_recv)
    stat_sems = (stat_out, stat_in, s_send, s_recv)
    query, query_wait = sender(*query_sems, -1), waiter(*query_sems)
    part, part_wait = sender(*part_sems, 1), waiter(*part_sems)
    stat, stat_wait = sender(*stat_sems, 1), waiter(*stat_sems)

    groups = OWNERS // BATCH

    def live(n, devices):
        return n * BATCH + jnp.where(n == 0, 1, 0), n * BATCH + (devices - n + STRIDE) // STRIDE

    def for_earlier(body):
        loop(0, groups, lambda n: body(n, *live(n, me)))

    def for_later(body):
        loop(0, groups, lambda n: body(n, *live(n, OWNERS - 1 - me)))

    def send_queries(j):
        for_earlier(lambda n, low, high: loop(low, high, lambda p: query(j, p).start()))

    def device(yy, zz, cc):
        return {"seq": (yy * 8 + zz) * 2 + cc}

    def w_unit(phase, h, p, c):
        if phase == 0:
            return full.at[y, p, c, h] if h == 0 else full.at[p, z, c, h]
        return full.at[p, :, c, h] if h == 0 else full.at[:, p, c, h]

    def w_move(phase, h, step, way):
        along_z = (h == 0) == (phase == 0)
        pos = z if along_z else y
        ahead = lax.rem(pos + 8 + way, 8)
        unit = w_unit(phase, h, lax.rem(pos - way * (step - 1) + 8, 8), core)
        to = device(y, ahead, core) if along_z else device(ahead, z, core)
        i = 0 if way > 0 else 1
        return move(unit, unit, w_send.at[phase, h, i, step - 1], w_recv.at[phase, h, i, step - 1], to)

    def sibling(h, p, c):
        unit = w_unit(1, h, p, c)
        return move(unit, unit, sib_send.at[h, p], sib_recv.at[h, p], device(y, z, 1 - core))

    def w_moves(phase, step):
        ways = (1, -1) if step < 4 else (1,)
        return [(h, way, w_move(phase, h, step, way)) for way in ways for h in range(2)]

    def w_start(phase, step):
        if phase == 1 and step == 1:
            for h in range(2):
                sibling(h, (y, z)[h], core).start()
        for _, _, copy in w_moves(phase, step):
            copy.start()

    def w_wait(phase, step):
        for h, way, copy in w_moves(phase, step):
            copy.wait_recv()
            if phase == 1:
                sibling(h, lax.rem((y, z)[h] - way * step + 8, 8), core).start()

    def w_next(phase, step):
        w_wait(phase, step)
        if step < 4:
            w_start(phase, step + 1)
        elif phase == 0:
            w_start(1, 1)

    def own(h):
        j = h // GROUP
        cols = slice(h * HEAD, (h + 1) * HEAD)
        for part_no in range(2):
            rows = slice(part_no * 256, part_no * 256 + 256)
            keys = (part_no + 1) * 256
            s = dot_t(q_ref[rows, cols], k_ref[0:keys, j * HEAD:(j + 1) * HEAD])
            seen = iota((256, keys), 1) <= iota((256, keys), 0) + part_no * 256
            s = jnp.where(seen, s, -1e30)
            peak = jnp.max(s, axis=1, keepdims=True)
            weights = jnp.exp2((s - peak) * SCALE)
            own_peak[rows, cols] = jnp.broadcast_to(peak * SCALE, (256, HEAD))
            own_total[rows, cols] = jnp.broadcast_to(jnp.sum(weights, axis=1, keepdims=True), (256, HEAD))
            own_out[rows, cols] = dot(weights.astype(BF16), v_ref[0:keys, j * HEAD:(j + 1) * HEAD])

    def remote(j, n):
        base = n * BATCH
        low, high = live(n, OWNERS - 1 - me)
        query_wait(j, n, low, high, False)
        batch = pl.ds(base, BATCH)
        rows = q_in[j, batch].astype(F32).reshape(BATCH * ROWS, HEAD).astype(BF16)
        s = dot_t(rows, k_ref[:, j * HEAD:(j + 1) * HEAD])
        peak = jnp.max(s, axis=1, keepdims=True)
        weights = jnp.exp2((s - peak) * SCALE)
        mass = jnp.sum(weights, axis=1, keepdims=True)
        mixed = dot(weights.astype(BF16), v_ref[:, j * HEAD:(j + 1) * HEAD]) * (1.0 / mass)
        part_out[j, batch] = mixed.reshape(BATCH, ROWS, HEAD).astype(BF16)
        level = peak * SCALE + jnp.log(mass) * LOG2E
        level = jnp.broadcast_to(level, (BATCH * ROWS, HEAD)).reshape(BATCH, ROWS, HEAD)
        diagonal = iota(level.shape, 1) == iota(level.shape, 2)
        stat_out[j, batch] = jnp.sum(jnp.where(diagonal, level, 0.0), axis=1, keepdims=True)

        def answer(d):
            part(j, d).start()
            stat(j, d).start()

        loop(low, high, answer)

    def remote_some(j, i, count):
        loop(groups * i // count, groups * (i + 1) // count, lambda n: remote(j, n))

    def combine(j):
        def arrived(n, low, high):
            part_wait(j, n, low, high, False)
            stat_wait(j, n, low, high, False)

        for_earlier(arrived)

        def widen(i):
            block = part_in[j, pl.ds(i * 16, 16)].astype(F32)
            gap = away(iota(block.shape, 0) + i * 16)
            block = jnp.where((gap > 0) & (gap <= me), block, 0.0)
            rows32[j, pl.ds(pl.multiple_of(i * 16 * ROWS, 16 * ROWS), 16 * ROWS), :] = block.reshape(16 * ROWS, HEAD)

        loop(0, OWNERS // 16, widen)
        levels = jnp.sum(stat_in[j], axis=1)
        gap = away(iota(levels.shape, 0))
        levels = jnp.where((gap > 0) & (gap <= me), levels, 0.0)
        high = levels.astype(BF16)
        rest = levels - high.astype(F32)
        mid = rest.astype(BF16)
        low = (rest - mid.astype(F32)).astype(BF16)
        found = [(dot(hits[...], piece) * ranked[...]).astype(BF16) for piece in (high, mid, low)]
        for pair in range(GROUP // 2):
            lane, head = iota((HEAD, 2 * HEAD), 0), iota((HEAD, 2 * HEAD), 1) // HEAD + 2 * pair
            spread = jnp.where((lane % GROUP == head) & (lane < ROWS), 1.0, 0.0).astype(BF16)
            source = jnp.concatenate([jnp.concatenate(
                [rows32[j, pl.ds(GROUP * r + 2 * pair + i, OWNERS, ROWS), :].astype(BF16) for i in range(2)],
                axis=1) for r in range(CAP)], axis=0)
            cols = slice((j * GROUP + 2 * pair) * HEAD, (j * GROUP + 2 * pair + 2) * HEAD)
            for half in range(2):
                rows = slice(half * 256, half * 256 + 256)
                got, level = [], []
                for c in range(2):
                    some = slice(c * BLOCK + half * 256, c * BLOCK + half * 256 + 256)
                    got.append(dot(choose[some], source))
                    level.append(sum(dot(piece[some], spread) for piece in found) + dead[some])
                peak = own_peak[rows, cols]
                top = jnp.maximum(peak, jnp.maximum(level[0], level[1]))
                own_share = jnp.exp2(peak - top)
                share = [jnp.exp2(level[c] - top) for c in range(2)]
                norm = 1.0 / (own_share * own_total[rows, cols] + share[0] + share[1])
                mixed = own_out[rows, cols] * own_share + got[0] * share[0] + got[1] * share[1]
                every[x, j, rows, 2 * pair * HEAD:(2 * pair + 2) * HEAD] = (mixed * norm).astype(BF16)

    upper, lower = pl.ds(0, BLOCK // 2), pl.ds(BLOCK // 2, BLOCK // 2)

    def x_move(j, i, owner, rows, to):
        unit = every.at[owner, j, rows]
        return move(unit, unit, x_send.at[j, i], x_recv.at[j, i], {"head": to})

    def x_copies(j):
        return [
            x_move(j, 0, x, upper, right), x_move(j, 1, x, lower, left),
            x_move(j, 2, x, lower, right), x_move(j, 3, x, upper, left),
        ]

    def x_onward(j):
        return [x_move(j, 4, left, upper, right), x_move(j, 5, right, lower, left)]

    def x_start(j):
        for copy in x_copies(j):
            copy.start()

    def x_forward(j):
        copies, onward = x_copies(j), x_onward(j)
        for i in range(2):
            copies[i].wait_recv()
            onward[i].start()

    def project(owner, j, first_term):
        a = every[owner, j]
        for n in range(4):
            cols = slice(n * 256, n * 256 + 256)
            w = full[2 * owner + j, :, :, :, :, cols].reshape(BLOCK, 256)
            term = dot(a, w)
            total[:, cols] = term if first_term else total[:, cols] + term

    def w_finish():
        for phase in range(2):
            for step in range(1, 5):
                for _, _, copy in w_moves(phase, step):
                    copy.wait_send()
        for h in range(2):
            for p in range(8):
                sibling(h, p, 1 - core).wait_recv()
                sibling(h, p, core).wait_send()

    def all_sent():
        def queries_sent(n, low, high):
            for j in range(KV):
                query_wait(j, n, low, high, True)

        def parts_sent(n, low, high):
            for j in range(KV):
                part_wait(j, n, low, high, True)
                stat_wait(j, n, low, high, True)

        for_earlier(queries_sent)
        for_later(parts_sent)

    gather(0)
    w_copy.wait()
    pl.semaphore_wait(barrier, OWNERS + 1)
    send_queries(0)
    w_start(0, 1)
    gather(1)
    send_queries(1)
    for i in range(4):
        remote_some(0, i, 4)
        w_next(0, i + 1)
    for i in range(4):
        remote_some(1, i, 4)
        own(2 * i)
        own(2 * i + 1)
        if i == 0:
            tables()
        if i in (1, 3):
            w_next(1, 1 + i // 2)
    combine(0)
    x_start(0)
    w_next(1, 3)
    x_forward(0)
    combine(1)
    x_start(1)
    w_wait(1, 4)
    w_finish()
    for copy in x_copies(0)[2:] + x_onward(0):
        copy.wait_recv()
    project(x, 0, True)
    project(left, 0, False)
    project(right, 0, False)
    x_forward(1)
    project(lax.rem(x + 2, 4), 0, False)
    project(x, 1, False)
    all_sent()
    for copy in x_copies(1)[2:]:
        copy.wait_recv()
    project(left, 1, False)
    project(right, 1, False)
    for copy in x_onward(1):
        copy.wait_recv()
    project(lax.rem(x + 2, 4), 1, False)
    out_ref[...] = total[...].astype(BF16)
    for j in range(KV):
        for copy in x_copies(j) + x_onward(j):
            copy.wait_send()


def on_device(queries, keys, values, picks, out_weight):
    vmem, dma = pltpu.VMEM, pltpu.SemaphoreType.DMA
    features = out_weight.shape[1]
    return pl.pallas_call(
        kernel,
        out_shape=jax.ShapeDtypeStruct((BLOCK, features), BF16),
        in_specs=[pl.BlockSpec(memory_space=vmem)] * 5,
        out_specs=pl.BlockSpec(memory_space=vmem),
        scratch_shapes=[
            vmem((KV, OWNERS * ROWS, HEAD), F32),
            vmem((KV, OWNERS, ROWS, HEAD), BF16),
            vmem((KV, OWNERS, ROWS, HEAD), BF16),
            vmem((KV, OWNERS, ROWS, HEAD), BF16),
            vmem((KV, OWNERS, ROWS, HEAD), BF16),
            vmem((KV, OWNERS, 1, HEAD), F32),
            vmem((KV, OWNERS, 1, HEAD), F32),
            vmem((BLOCK, KV * GROUP * HEAD), F32),
            vmem((BLOCK, KV * GROUP * HEAD), F32),
            vmem((BLOCK, KV * GROUP * HEAD), F32),
            vmem((2 * BLOCK, SLOTS), BF16),
            vmem((2 * BLOCK, OWNERS), BF16),
            vmem((2 * BLOCK, OWNERS), F32),
            vmem((2 * BLOCK, 2 * HEAD), F32),
            vmem((8, 8, 2, 2, 16, features), BF16),
            vmem((4, KV, BLOCK, GROUP * HEAD), BF16),
            vmem((BLOCK, features), F32),
            dma((KV, OWNERS // BATCH)), dma((KV, OWNERS // BATCH)),
            dma((KV, OWNERS // BATCH)), dma((KV, OWNERS // BATCH)),
            dma((KV, OWNERS // BATCH)), dma((KV, OWNERS // BATCH)),
            dma, dma((2, 2, 2, 4)), dma((2, 2, 2, 4)), dma((2, 8)), dma((2, 8)),
            dma((KV, 6)), dma((KV, 6)),
        ],
        compiler_params=pltpu.CompilerParams(
            collective_id=0, has_side_effects=True, vmem_limit_bytes=58 << 20
        ),
        cost_estimate=pl.CostEstimate(flops=7 << 30, bytes_accessed=4 << 20, transcendentals=5 << 20),
    )(queries, keys, values, picks.T, out_weight.reshape(2, 16, features))


def solution(mesh):
    return jax.shard_map(
        on_device,
        mesh=mesh,
        in_specs=(
            P("seq", "head"),
            P("seq", "head"),
            P("seq", "head"),
            P("seq", None),
            P("seq", "head"),
        ),
        out_specs=P("seq", "head"),
        check_vma=False,
    )
```

```python
import functools
import math

import jax
import jax.numpy as jnp
from jax import lax
from jax.experimental import pallas as pl
from jax.experimental.pallas import tpu as pltpu
from jax.sharding import PartitionSpec as P

HEAD = 128
CAP = 6
BLOCK = 512
OWNERS = 128
GROUP = 4
KV = 2
ROWS = CAP * GROUP
SLOTS = CAP * OWNERS
BATCH = 8
STRIDE = OWNERS // BATCH
MESH = pl.DeviceIdType.MESH
F32 = jnp.float32
BF16 = jnp.bfloat16
LOG2E = 1.0 / math.log(2.0)
SCALE = LOG2E / math.sqrt(HEAD)


def dot(a, b):
    return lax.dot_general(a, b, (((1,), (0,)), ((), ())), preferred_element_type=F32)


def dot_t(a, b):
    return lax.dot_general(a, b, (((1,), (1,)), ((), ())), preferred_element_type=F32)


def loop(low, high, body):
    def step(i, carry):
        body(i)
        return carry

    lax.fori_loop(low, high, step, 0)


def iota(shape, dim):
    return lax.broadcasted_iota(jnp.int32, shape, dim)


def kernel(
    q_ref, k_ref, v_ref, picks_ref, w_ref, out_ref,
    rows32, q_out, q_in, part_out, part_in, stat_out, stat_in,
    own_out, own_peak, own_total, choose, hits, ranked, dead, full, every, total,
    q_send, q_recv, p_send, p_recv, s_send, s_recv,
    w_local, w_send, w_recv, sib_send, sib_recv, x_send, x_recv,
):
    me = lax.axis_index("seq")
    x = lax.axis_index("head")
    core = lax.rem(me, 2)
    z = lax.rem(me // 2, 8)
    y = me // 16
    right, left = lax.rem(x + 1, 4), lax.rem(x + 3, 4)

    barrier = pltpu.get_barrier_semaphore()
    loop(1, OWNERS, lambda i: pl.semaphore_signal(
        barrier, inc=1, device_id={"seq": lax.rem(me + i, OWNERS)}, device_id_type=MESH))
    for friend in (right, left):
        pl.semaphore_signal(barrier, inc=1, device_id={"head": friend}, device_id_type=MESH)

    w_copy = pltpu.make_async_copy(w_ref, full.at[y, z, core], w_local)
    w_copy.start()

    def away(p):
        return STRIDE * (p % BATCH) + p // BATCH

    def place_of(block):
        return (me - block) % STRIDE * BATCH + (me - block) // STRIDE

    first, second = picks_ref[0:1, :], picks_ref[1:2, :]
    places = iota((OWNERS, BLOCK), 0)
    owners = me - away(places)
    owners = jnp.where(owners < 0, -2, owners)
    hit0, hit1 = first == owners, second == owners
    named = jnp.where(hit0 | hit1, 1.0, 0.0).astype(BF16)
    before = jnp.where(iota((BLOCK, BLOCK), 0) < iota((BLOCK, BLOCK), 1), 1.0, 0.0).astype(BF16)
    rank = dot(named, before)
    rank0 = jnp.sum(jnp.where(hit0, rank, 0.0), axis=0, keepdims=True)
    rank1 = jnp.sum(jnp.where(hit1, rank, 0.0), axis=0, keepdims=True)
    slot0 = jnp.where(first >= 0, rank0.astype(jnp.int32) * OWNERS + place_of(first), -1)
    slot1 = jnp.where(second >= 0, rank1.astype(jnp.int32) * OWNERS + place_of(second), -1)

    def gather(j):
        for r in range(CAP):
            at = places + r * OWNERS
            pick = jnp.where((slot0 == at) | (slot1 == at), 1.0, 0.0).astype(BF16)
            got = dot(pick, q_ref[:, j * GROUP * HEAD:(j + 1) * GROUP * HEAD])
            for g in range(GROUP):
                rows32[j, pl.ds(GROUP * r + g, OWNERS, ROWS), :] = got[:, g * HEAD:(g + 1) * HEAD]

        def pack(i):
            block = rows32[j, pl.ds(pl.multiple_of(i * 16 * ROWS, 16 * ROWS), 16 * ROWS), :]
            q_out[j, pl.ds(i * 16, 16)] = block.reshape(16, ROWS, HEAD).astype(BF16)

        loop(0, OWNERS // 16, pack)

    def tables():
        line = iota((OWNERS, BLOCK), 0)
        flat = jnp.where(line == 0, first.astype(F32), jnp.where(line == 1, second.astype(F32),
               jnp.where(line == 2, rank0, jnp.where(line == 3, rank1, 0.0))))
        columns = jnp.transpose(flat)
        lane = iota((BLOCK, OWNERS), 1)
        for c in range(2):
            rows = slice(c * BLOCK, (c + 1) * BLOCK)
            name = columns[:, c:c + 1].astype(jnp.int32)
            rank = columns[:, c + 2:c + 3].astype(jnp.int32)
            place = jnp.where(name >= 0, place_of(name), -1)
            slot = jnp.where(name >= 0, rank * OWNERS + place, -1)
            for r in range(CAP):
                choose[rows, r * OWNERS:(r + 1) * OWNERS] = jnp.where(slot == lane + r * OWNERS, 1.0, 0.0).astype(BF16)
            hits[rows] = jnp.where(place == lane, 1.0, 0.0).astype(BF16)
            ranked[rows] = jnp.where(rank == lane // GROUP, 1.0, 0.0)
            dead[rows] = jnp.where(jnp.broadcast_to(name, (BLOCK, 2 * HEAD)) >= 0, 0.0, -1e30)

    def move(src, dst, send_sem, recv_sem, to):
        return pltpu.make_async_remote_copy(
            src_ref=src, dst_ref=dst, send_sem=send_sem, recv_sem=recv_sem,
            device_id=to, device_id_type=MESH)

    def sender(out, into, send, recv, way):
        def copy(j, p):
            return move(out.at[j, p], into.at[j, p], send.at[j, p // BATCH], recv.at[j, p // BATCH],
                        {"seq": me + way * away(p)})
        return copy

    def waiter(out, into, send, recv):
        def wait(j, n, low, high, sent):
            for count in range(1, BATCH + 1):
                @pl.when(high - low == count)
                def _():
                    some = pl.ds(low, count)
                    copy = move(out.at[j, some], into.at[j, some], send.at[j, n], recv.at[j, n],
                                {"seq": lax.rem(me + 1, OWNERS)})
                    if sent:
                        copy.wait_send()
                    else:
                        copy.wait_recv()
        return wait

    query_sems = (q_out, q_in, q_send, q_recv)
    part_sems = (part_out, part_in, p_send, p_recv)
    stat_sems = (stat_out, stat_in, s_send, s_recv)
    query, query_wait = sender(*query_sems, -1), waiter(*query_sems)
    part, part_wait = sender(*part_sems, 1), waiter(*part_sems)
    stat, stat_wait = sender(*stat_sems, 1), waiter(*stat_sems)

    groups = OWNERS // BATCH

    def live(n, devices):
        return n * BATCH + jnp.where(n == 0, 1, 0), n * BATCH + (devices - n + STRIDE) // STRIDE

    def for_earlier(body):
        loop(0, groups, lambda n: body(n, *live(n, me)))

    def for_later(body):
        loop(0, groups, lambda n: body(n, *live(n, OWNERS - 1 - me)))

    def send_queries(j):
        for_earlier(lambda n, low, high: loop(low, high, lambda p: query(j, p).start()))

    def device(yy, zz, cc):
        return {"seq": (yy * 8 + zz) * 2 + cc}

    def w_unit(phase, h, p, c):
        if phase == 0:
            return full.at[y, p, c, h] if h == 0 else full.at[p, z, c, h]
        return full.at[p, :, c, h] if h == 0 else full.at[:, p, c, h]

    def w_move(phase, h, step, way):
        along_z = (h == 0) == (phase == 0)
        pos = z if along_z else y
        ahead = lax.rem(pos + 8 + way, 8)
        unit = w_unit(phase, h, lax.rem(pos - way * (step - 1) + 8, 8), core)
        to = device(y, ahead, core) if along_z else device(ahead, z, core)
        i = 0 if way > 0 else 1
        return move(unit, unit, w_send.at[phase, h, i, step - 1], w_recv.at[phase, h, i, step - 1], to)

    def sibling(h, p, c):
        unit = w_unit(1, h, p, c)
        return move(unit, unit, sib_send.at[h, p], sib_recv.at[h, p], device(y, z, 1 - core))

    def w_moves(phase, step):
        ways = (1, -1) if step < 4 else (1,)
        return [(h, way, w_move(phase, h, step, way)) for way in ways for h in range(2)]

    def w_start(phase, step):
        if phase == 1 and step == 1:
            for h in range(2):
                sibling(h, (y, z)[h], core).start()
        for _, _, copy in w_moves(phase, step):
            copy.start()

    def w_wait(phase, step):
        for h, way, copy in w_moves(phase, step):
            copy.wait_recv()
            if phase == 1:
                sibling(h, lax.rem((y, z)[h] - way * step + 8, 8), core).start()

    def w_next(phase, step):
        w_wait(phase, step)
        if step < 4:
            w_start(phase, step + 1)
        elif phase == 0:
            w_start(1, 1)

    def own(h):
        j = h // GROUP
        cols = slice(h * HEAD, (h + 1) * HEAD)
        for part_no in range(2):
            rows = slice(part_no * 256, part_no * 256 + 256)
            keys = (part_no + 1) * 256
            s = dot_t(q_ref[rows, cols], k_ref[0:keys, j * HEAD:(j + 1) * HEAD])
            seen = iota((256, keys), 1) <= iota((256, keys), 0) + part_no * 256
            s = jnp.where(seen, s, -1e30)
            peak = jnp.max(s, axis=1, keepdims=True)
            weights = jnp.exp2((s - peak) * SCALE)
            own_peak[rows, cols] = jnp.broadcast_to(peak * SCALE, (256, HEAD))
            own_total[rows, cols] = jnp.broadcast_to(jnp.sum(weights, axis=1, keepdims=True), (256, HEAD))
            own_out[rows, cols] = dot(weights.astype(BF16), v_ref[0:keys, j * HEAD:(j + 1) * HEAD])

    def remote(j, n):
        base = n * BATCH
        low, high = live(n, OWNERS - 1 - me)
        query_wait(j, n, low, high, False)
        batch = pl.ds(base, BATCH)
        rows = q_in[j, batch].astype(F32).reshape(BATCH * ROWS, HEAD).astype(BF16)
        s = dot_t(rows, k_ref[:, j * HEAD:(j + 1) * HEAD])
        peak = jnp.max(s, axis=1, keepdims=True)
        weights = jnp.exp2((s - peak) * SCALE)
        mass = jnp.sum(weights, axis=1, keepdims=True)
        mixed = dot(weights.astype(BF16), v_ref[:, j * HEAD:(j + 1) * HEAD]) * (1.0 / mass)
        part_out[j, batch] = mixed.reshape(BATCH, ROWS, HEAD).astype(BF16)
        level = peak * SCALE + jnp.log(mass) * LOG2E
        level = jnp.broadcast_to(level, (BATCH * ROWS, HEAD)).reshape(BATCH, ROWS, HEAD)
        diagonal = iota(level.shape, 1) == iota(level.shape, 2)
        stat_out[j, batch] = jnp.sum(jnp.where(diagonal, level, 0.0), axis=1, keepdims=True)

        def answer(d):
            part(j, d).start()
            stat(j, d).start()

        loop(low, high, answer)

    def remote_some(j, i, count):
        loop(groups * i // count, groups * (i + 1) // count, lambda n: remote(j, n))

    upper, lower = pl.ds(0, BLOCK // 2), pl.ds(BLOCK // 2, BLOCK // 2)

    def x_move(j, pair, i, owner, rows, to):
        unit = every.at[owner, j, rows, pl.ds(2 * pair * HEAD, 2 * HEAD)]
        return move(unit, unit, x_send.at[j, pair, i], x_recv.at[j, pair, i], {"head": to})

    def x_first(j, pair):
        return [x_move(j, pair, 0, x, upper, right), x_move(j, pair, 1, x, lower, left)]

    def x_second(j, pair):
        return [x_move(j, pair, 2, x, lower, right), x_move(j, pair, 3, x, upper, left)]

    def x_onward(j, pair):
        return [x_move(j, pair, 4, left, upper, right), x_move(j, pair, 5, right, lower, left)]

    def x_start(j, pair):
        for copy in x_first(j, pair) + x_second(j, pair):
            copy.start()

    def x_forward(j):
        for pair in range(2):
            for here, onward in zip(x_first(j, pair), x_onward(j, pair)):
                here.wait_recv()
                onward.start()

    def combine(j):
        def arrived(n, low, high):
            part_wait(j, n, low, high, False)
            stat_wait(j, n, low, high, False)

        for_earlier(arrived)

        def widen(i):
            block = part_in[j, pl.ds(i * 16, 16)].astype(F32)
            gap = away(iota(block.shape, 0) + i * 16)
            block = jnp.where((gap > 0) & (gap <= me), block, 0.0)
            rows32[j, pl.ds(pl.multiple_of(i * 16 * ROWS, 16 * ROWS), 16 * ROWS), :] = block.reshape(16 * ROWS, HEAD)

        loop(0, OWNERS // 16, widen)
        levels = jnp.sum(stat_in[j], axis=1)
        gap = away(iota(levels.shape, 0))
        levels = jnp.where((gap > 0) & (gap <= me), levels, 0.0)
        high = levels.astype(BF16)
        rest = levels - high.astype(F32)
        mid = rest.astype(BF16)
        low = (rest - mid.astype(F32)).astype(BF16)
        found = [(dot(hits[...], piece) * ranked[...]).astype(BF16) for piece in (high, mid, low)]
        for pair in range(GROUP // 2):
            lane, head = iota((HEAD, 2 * HEAD), 0), iota((HEAD, 2 * HEAD), 1) // HEAD + 2 * pair
            spread = jnp.where((lane % GROUP == head) & (lane < ROWS), 1.0, 0.0).astype(BF16)
            source = jnp.concatenate([jnp.concatenate(
                [rows32[j, pl.ds(GROUP * r + 2 * pair + i, OWNERS, ROWS), :].astype(BF16) for i in range(2)],
                axis=1) for r in range(CAP)], axis=0)
            cols = slice((j * GROUP + 2 * pair) * HEAD, (j * GROUP + 2 * pair + 2) * HEAD)
            for half in range(2):
                rows = slice(half * 256, half * 256 + 256)
                got, level = [], []
                for c in range(2):
                    some = slice(c * BLOCK + half * 256, c * BLOCK + half * 256 + 256)
                    got.append(dot(choose[some], source))
                    level.append(sum(dot(piece[some], spread) for piece in found) + dead[some])
                peak = own_peak[rows, cols]
                top = jnp.maximum(peak, jnp.maximum(level[0], level[1]))
                own_share = jnp.exp2(peak - top)
                share = [jnp.exp2(level[c] - top) for c in range(2)]
                norm = 1.0 / (own_share * own_total[rows, cols] + share[0] + share[1])
                mixed = own_out[rows, cols] * own_share + got[0] * share[0] + got[1] * share[1]
                every[x, j, rows, 2 * pair * HEAD:(2 * pair + 2) * HEAD] = (mixed * norm).astype(BF16)
            x_start(j, pair)

    def project(owner, j, first_term):
        a = every[owner, j]
        for n in range(4):
            cols = slice(n * 256, n * 256 + 256)
            w = full[2 * owner + j, :, :, :, :, cols].reshape(BLOCK, 256)
            term = dot(a, w)
            total[:, cols] = term if first_term else total[:, cols] + term

    def w_finish():
        for phase in range(2):
            for step in range(1, 5):
                for _, _, copy in w_moves(phase, step):
                    copy.wait_send()
        for h in range(2):
            for p in range(8):
                sibling(h, p, 1 - core).wait_recv()
                sibling(h, p, core).wait_send()

    def all_sent():
        def queries_sent(n, low, high):
            for j in range(KV):
                query_wait(j, n, low, high, True)

        def parts_sent(n, low, high):
            for j in range(KV):
                part_wait(j, n, low, high, True)
                stat_wait(j, n, low, high, True)

        for_earlier(queries_sent)
        for_later(parts_sent)

    gather(0)
    w_copy.wait()
    pl.semaphore_wait(barrier, OWNERS + 1)
    send_queries(0)
    w_start(0, 1)
    gather(1)
    send_queries(1)
    for i in range(4):
        remote_some(0, i, 4)
        w_next(0, i + 1)
    for i in range(4):
        remote_some(1, i, 4)
        own(2 * i)
        own(2 * i + 1)
        if i == 0:
            tables()
        if i in (1, 3):
            w_next(1, 1 + i // 2)
    combine(0)
    w_next(1, 3)
    x_forward(0)
    combine(1)
    w_wait(1, 4)
    w_finish()
    for pair in range(2):
        for copy in x_second(0, pair) + x_onward(0, pair):
            copy.wait_recv()
    project(x, 0, True)
    project(left, 0, False)
    project(right, 0, False)
    x_forward(1)
    project(lax.rem(x + 2, 4), 0, False)
    project(x, 1, False)
    all_sent()
    for pair in range(2):
        for copy in x_second(1, pair):
            copy.wait_recv()
    project(left, 1, False)
    project(right, 1, False)
    for pair in range(2):
        for copy in x_onward(1, pair):
            copy.wait_recv()
    project(lax.rem(x + 2, 4), 1, False)
    out_ref[...] = total[...].astype(BF16)
    for j in range(KV):
        for pair in range(2):
            for copy in x_first(j, pair) + x_second(j, pair) + x_onward(j, pair):
                copy.wait_send()


def on_device(queries, keys, values, picks, out_weight):
    vmem, dma = pltpu.VMEM, pltpu.SemaphoreType.DMA
    features = out_weight.shape[1]
    return pl.pallas_call(
        kernel,
        out_shape=jax.ShapeDtypeStruct((BLOCK, features), BF16),
        in_specs=[pl.BlockSpec(memory_space=vmem)] * 5,
        out_specs=pl.BlockSpec(memory_space=vmem),
        scratch_shapes=[
            vmem((KV, OWNERS * ROWS, HEAD), F32),
            vmem((KV, OWNERS, ROWS, HEAD), BF16),
            vmem((KV, OWNERS, ROWS, HEAD), BF16),
            vmem((KV, OWNERS, ROWS, HEAD), BF16),
            vmem((KV, OWNERS, ROWS, HEAD), BF16),
            vmem((KV, OWNERS, 1, HEAD), F32),
            vmem((KV, OWNERS, 1, HEAD), F32),
            vmem((BLOCK, KV * GROUP * HEAD), F32),
            vmem((BLOCK, KV * GROUP * HEAD), F32),
            vmem((BLOCK, KV * GROUP * HEAD), F32),
            vmem((2 * BLOCK, SLOTS), BF16),
            vmem((2 * BLOCK, OWNERS), BF16),
            vmem((2 * BLOCK, OWNERS), F32),
            vmem((2 * BLOCK, 2 * HEAD), F32),
            vmem((8, 8, 2, 2, 16, features), BF16),
            vmem((4, KV, BLOCK, GROUP * HEAD), BF16),
            vmem((BLOCK, features), F32),
            dma((KV, OWNERS // BATCH)), dma((KV, OWNERS // BATCH)),
            dma((KV, OWNERS // BATCH)), dma((KV, OWNERS // BATCH)),
            dma((KV, OWNERS // BATCH)), dma((KV, OWNERS // BATCH)),
            dma, dma((2, 2, 2, 4)), dma((2, 2, 2, 4)), dma((2, 8)), dma((2, 8)),
            dma((KV, 2, 6)), dma((KV, 2, 6)),
        ],
        compiler_params=pltpu.CompilerParams(
            collective_id=0, has_side_effects=True, vmem_limit_bytes=58 << 20
        ),
        cost_estimate=pl.CostEstimate(flops=7 << 30, bytes_accessed=4 << 20, transcendentals=5 << 20),
    )(queries, keys, values, picks.T, out_weight.reshape(2, 16, features))


def solution(mesh):
    return jax.shard_map(
        on_device,
        mesh=mesh,
        in_specs=(
            P("seq", "head"),
            P("seq", "head"),
            P("seq", "head"),
            P("seq", None),
            P("seq", "head"),
        ),
        out_specs=P("seq", "head"),
        check_vma=False,
    )
```
